512 devices in a mesh: pipe: 32 (over y_hi, z), expert: 16 (over x, y_lo, core).
Axes of the slice: x: 4, y: 4 (y_hi: 2, y_lo: 2; y = y_hi * 2 + y_lo), z: 16, core: 2. Of those that a mesh axis runs over, the one named last changes fastest.
Arguments:
- grad_out: bfloat16 [2, 32768, 3584], P(None, ('pipe', 'expert')), may hold values from -6 to 6
- route_slot: int32 [2, 32768], P(None, ('pipe', 'expert')), may hold values from -1 to 39, as said below
- gate_weight: float32 [2, 32768], P(None, ('pipe', 'expert')), may hold values from 0.3 to 1.5
- stored_pre: bfloat16 [32, 16, 40, 2, 2048], P('pipe', None, None, None, 'expert'), may hold values from -6 to 6
- w_in: bfloat16 [32, 2048, 2, 3584], P('pipe', 'expert'), may hold values from -0.09375 to 0.09375
- w_out: bfloat16 [32, 2048, 3584], P('pipe', 'expert'), may hold values from -0.1875 to 0.1875
Outputs:
- received: bfloat16 [2, 32768, 3584], P(None, ('pipe', 'expert'))
The draws below stay inside these ranges and needn't reach their ends.
Inputs may be any that keep to these rules, and one draw needn't show every extreme that they name: `route_slot`: in each device's block of 64 tokens of one direction exactly 40 tokens carry a slot, each slot 0 to 39 taken once; the other tokens carry -1.
All inputs are finite; a program needn't handle non-finite values.
Results may differ from the reference program's by a relative error of at most 0.0054.
Values may be sent and summed in bfloat16 or wider, within the bound.
A program may use at most 64 MiB of HBM per device.

```python
import jax
import jax.numpy as jnp
from jax import lax

D = 3584
FH = 1024
TOK_DEV = 64
CAP = 40
TOKENS = 32768
N_PIPE = 32
N_EXPERT = 16


def draw_route_slot(key, part):
    key = jax.random.fold_in(key, 5)
    blocks = 2 * TOKENS // TOK_DEV
    keys = jax.random.split(key, blocks)
    order = jax.vmap(lambda sub_key: jax.random.permutation(sub_key, TOK_DEV))(keys).astype(jnp.int32)
    chosen = jnp.where(order < CAP, order, -1)
    return chosen.reshape(2, TOKENS).astype(jnp.int32)


def block_levels(rng, shape, pieces, least, high):
    def one(dim, blocks):
        heights = jax.random.uniform(jax.random.fold_in(jax.random.fold_in(rng, 6), dim), (blocks,), jnp.float32, least / len(pieces), high / len(pieces))
        return jnp.repeat(jnp.exp(heights), shape[dim] // blocks).reshape((-1,) + (1,) * (len(shape) - dim - 1))

    gain = one(*pieces[0])
    for cut in pieces[1:]:
        gain = gain * one(*cut)
    return gain


def bell_draw(key, extent, scale, bound, cuts=(), kind=jnp.bfloat16):
    array = jax.random.normal(key, extent, jnp.float32) * scale
    if len(cuts) > 0:
        array = block_levels(key, extent, cuts, -0.22, 0.18) * array
    return jnp.clip(array, min=-bound, max=bound).astype(kind)


def setup_inputs(seed: int = 0) -> dict:
    key_of = jax.random.split(jax.random.key(seed), 7)
    grad_out = bell_draw(key_of[0], (2, TOKENS, D), 1.0, 6.0, ((1, 512),))
    route_slot = draw_route_slot(jax.random.fold_in(key_of[6], 71), 0)
    gate_weight = jnp.clip(0.3 + 1.2 * jax.random.uniform(key_of[2], (2, TOKENS), jnp.float32) ** block_levels(key_of[2], (2, TOKENS), ((1, 512),), -0.2, 0.2), 0.3, 1.5)
    stored_pre = bell_draw(key_of[3], (N_PIPE, N_EXPERT, CAP, 2, 2 * FH), 1.5, 6.0, ((0, 32), (4, 16)))
    w_in = bell_draw(key_of[4], (N_PIPE, 2 * FH, 2, D), D ** -0.5, 0.09375, ((0, 32), (1, 16)))
    w_out = bell_draw(key_of[5], (N_PIPE, 2 * FH, D), FH ** -0.5, 0.1875, ((0, 32), (1, 16)))
    return dict(grad_out=grad_out, route_slot=route_slot, gate_weight=gate_weight, stored_pre=stored_pre, w_in=w_in, w_out=w_out)


def swiglu_back(hidden_grad, gate_pre, up_pre):
    gate_pre = gate_pre.astype(jnp.float32)
    up_pre = up_pre.astype(jnp.float32)
    squashed = jax.nn.sigmoid(gate_pre)
    gate_grad = hidden_grad * up_pre * squashed * (1.0 + gate_pre * (1.0 - squashed))
    up_grad = hidden_grad * gate_pre * squashed
    return jnp.stack([gate_grad, up_grad], axis=-1)


def rank_direction(gradient, slot_rows, gate_rows, stored_rank, weight_in, weight_out):
    onehot = (slot_rows[:, :, None] == jnp.arange(CAP, dtype=jnp.int32)[None, None, :]).astype(jnp.float32)
    scaled = (gate_rows[:, :, None] * gradient.astype(jnp.float32)).astype(jnp.bfloat16)
    arrived = jnp.einsum("etc,etd->ecd", onehot, scaled.astype(jnp.float32)).astype(jnp.bfloat16)
    hidden_grad = jnp.einsum("ecd,fd->ecf", arrived.astype(jnp.float32), weight_out.astype(jnp.float32))
    pre_grad = swiglu_back(hidden_grad, stored_rank[:, :, 0], stored_rank[:, :, 1]).astype(jnp.bfloat16)
    slices = N_EXPERT // 2
    hidden_width = FH // slices
    pre_grad = lax.optimization_barrier(pre_grad).reshape(N_EXPERT, CAP, slices, 2 * hidden_width)
    grouped = weight_in.reshape(slices, 2 * hidden_width, D)
    partial_value = jnp.einsum("ecqj,qjd->qecd", pre_grad.astype(jnp.float32), grouped.astype(jnp.float32)).astype(jnp.bfloat16)
    partial_value = lax.optimization_barrier(partial_value)
    expert_sum = jnp.sum(partial_value.astype(jnp.float32), axis=0)
    slot_index = jnp.clip(slot_rows, 0, CAP - 1).astype(jnp.int32)
    picked = jax.vmap(lambda table, where_from: table[where_from])(expert_sum, slot_index)
    contrib = jnp.where(slot_rows[:, :, None] >= 0, picked, jnp.float32(0.0))
    return (gradient.astype(jnp.float32) + contrib).astype(jnp.bfloat16)


def reference(grad_out, route_slot, gate_weight, stored_pre, w_in, w_out):
    block_rows = N_EXPERT * TOK_DEV

    def one_rank(rank):
        start = (rank * block_rows).astype(jnp.int32)
        stored_here = lax.dynamic_index_in_dim(stored_pre, rank, 0, keepdims=False)
        in_here = lax.dynamic_index_in_dim(w_in, rank, 0, keepdims=False)
        out_here = lax.dynamic_index_in_dim(w_out, rank, 0, keepdims=False)
        results = []
        for direction in range(2):
            gradient = lax.dynamic_slice_in_dim(grad_out[direction], start, block_rows, 0).reshape(N_EXPERT, TOK_DEV, D)
            slot_rows = lax.dynamic_slice_in_dim(route_slot[direction], start, block_rows, 0).reshape(N_EXPERT, TOK_DEV)
            gate_rows = lax.dynamic_slice_in_dim(gate_weight[direction], start, block_rows, 0).reshape(N_EXPERT, TOK_DEV)
            stored_rank = stored_here[:, :, :, direction * FH:(direction + 1) * FH]
            weight_in = in_here[direction * FH:(direction + 1) * FH]
            weight_out = out_here[direction * FH:(direction + 1) * FH]
            results.append(rank_direction(gradient, slot_rows, gate_rows, stored_rank, weight_in, weight_out))
        return jnp.stack(results)

    layer_grad = lax.map(one_rank, jnp.arange(N_PIPE, dtype=jnp.int32))
    layer_grad = layer_grad.reshape(N_PIPE, 2, block_rows, D)
    empty_rank = jnp.zeros((1, block_rows, D), jnp.bfloat16)
    downward = jnp.concatenate([layer_grad[1:, 0], empty_rank], axis=0)
    upward = jnp.concatenate([empty_rank, layer_grad[:-1, 1]], axis=0)
    return jnp.stack([downward, upward]).reshape(2, N_PIPE * block_rows, D)
```

```python
import functools

import jax
import jax.numpy as jnp
from jax import lax
from jax.experimental import pallas as pl
from jax.experimental.pallas import tpu as pltpu
from jax.sharding import PartitionSpec as P

MESH = pl.DeviceIdType.MESH
F32, BF16 = jnp.float32, jnp.bfloat16
BLOCKS = [(c, f, s) for c in range(2) for f in range(2) for s in range(2)]


def number(block):
    return block[0] * 4 + block[1] * 2 + block[2]


def iota(shape, dim):
    return lax.broadcasted_iota(jnp.int32, shape, dim).astype(F32)


def kernel(
    n_pipe, capacity,
    grad_hbm, slot_ref, gate_ref, stored_hbm, w_in_hbm, w_out_hbm,
    out_hbm,
    grad_full, grad_chip, meta, w_out_chip, w_in_chip, stored_chip,
    raw, cross_block, x_block, hid_send, hid_recv, acc, ret_send, ret_sec,
    first_send, ret_first, cut_send, ret_cut, final, early, landed, out_buf,
    local_sem, send_sem, recv_sem,
):
    tokens, features = grad_full.shape[1:]
    half = features // 2
    p, e = lax.axis_index("pipe"), lax.axis_index("expert")
    core, y, x = e % 2, (e // 2) % 2, e // 4
    g = x // 2
    sibling = e + 1 - 2 * core
    x_next = e + 4 - 8 * (x % 2)
    y_next = e + 2 - 4 * y
    cut = e + 4 * (3 - 2 * x)
    first = x_next + core * (y_next - x_next)
    second = y_next + core * (x_next - y_next)
    base = e - core
    z_to = [p - 1 + 2 * g, p + 1 - 2 * g]
    z_from = [z_to[1], z_to[0]]

    def valid(rank):
        return jnp.logical_and(rank >= 0, rank < n_pipe)

    counter = [0]

    def take():
        counter[0] += 1
        return counter[0] - 1

    def remote(src, dst, device, index=None):
        index = take() if index is None else index
        return pltpu.make_async_remote_copy(
            src_ref=src, dst_ref=dst, send_sem=send_sem.at[index], recv_sem=recv_sem.at[index],
            device_id=device, device_id_type=MESH,
        )

    barrier = pltpu.get_barrier_semaphore()
    for other in (sibling, first, second, cut):
        pl.semaphore_signal(barrier, inc=1, device_id=(p, other), device_id_type=MESH)
    for rank in z_to:
        @pl.when(valid(rank))
        def _():
            for k in range(2):
                pl.semaphore_signal(barrier, inc=1, device_id=(rank, base + k), device_id_type=MESH)

    mine = pl.multiple_of(core * half, 128)
    theirs = pl.multiple_of((1 - core) * half, 128)

    def local(src, dst, index):
        return pltpu.make_async_copy(src, dst, local_sem.at[index])

    load_full = local(grad_hbm, grad_full, 0)
    load_half = local(grad_hbm.at[:, :, pl.ds(mine, half)], grad_chip.at[core], 1)
    load_out = local(w_out_hbm.at[:, pl.ds(mine, half)], w_out_chip.at[core], 2)
    load_in = local(w_in_hbm.at[:, :, pl.ds(mine, half)], w_in_chip.at[core], 3)
    load_stored = local(stored_hbm, stored_chip.at[core], 4)
    load_half.start()
    load_full.start()

    slot = slot_ref[...].astype(F32)
    gate = gate_ref[...]
    meta[0] = jnp.zeros_like(meta[0])
    meta[0, 0:2, 0:tokens] = slot
    meta[0, 0:2, tokens:2 * tokens] = slot
    meta[0, 2:4, 0:tokens] = gate
    meta[0, 2:4, tokens:2 * tokens] = gate

    pl.semaphore_wait(barrier, 4 + 2 * sum(valid(rank).astype(jnp.int32) for rank in z_to))

    pending = []

    def go(copy):
        copy.start()
        pending.append(copy)
        return copy

    got_meta = go(remote(meta.at[0], meta.at[1], (p, sibling)))
    got_grad = go(remote(
        grad_hbm.at[:, :, pl.ds(theirs, half)], grad_chip.at[core], (p, sibling)))
    load_out.start()
    load_stored.start()
    load_in.start()
    got_out = go(remote(w_out_hbm.at[:, pl.ds(theirs, half)], w_out_chip.at[core], (p, sibling)))
    got_stored = go(remote(stored_hbm, stored_chip.at[core], (p, sibling)))
    got_in = go(remote(w_in_hbm.at[:, :, pl.ds(theirs, half)], w_in_chip.at[core], (p, sibling)))

    load_half.wait()
    got_meta.wait_recv()
    got_grad.wait_recv()

    rows = 2 * capacity
    lane = lax.broadcasted_iota(jnp.int32, (1, 2 * tokens), 1)

    def pack(direction):
        own_slot = meta[0, pl.ds(direction, 1), :]
        sib_slot = meta[1, pl.ds(direction, 1), :]
        own_gate = meta[0, pl.ds(direction + 2, 1), :]
        sib_gate = meta[1, pl.ds(direction + 2, 1), :]
        is_own = (lane // tokens) == core
        chip_slot = jnp.where(is_own, own_slot, sib_slot)
        chip_gate = jnp.where(is_own, own_gate, sib_gate)
        chip_slot = jnp.where(
            jnp.logical_and(lane >= tokens, chip_slot >= 0), chip_slot + capacity, chip_slot)
        onehot = jnp.where(iota((rows, 2 * tokens), 0) == chip_slot, 1.0, 0.0)
        slot_gate = jnp.sum(onehot * chip_gate, axis=1, keepdims=True)
        both = jnp.concatenate([grad_chip[0, direction], grad_chip[1, direction]], axis=0)
        picked = jnp.dot(onehot.astype(BF16), both, preferred_element_type=F32)
        return picked.astype(BF16), (slot_gate * picked).astype(BF16)

    raw[1], cross_block[...] = pack(1 - g)
    got_x = {}
    got_x[1, 0, 0] = go(remote(cross_block, x_block.at[number((1, 0, 0))], (p, cut)))
    raw[0], x_block[0] = pack(g)

    def forward(block, along):
        c, f, s = block
        target = (c, 1, s) if along == "first" else (c, f, 1)
        device = first if along == "first" else second
        got_x[target] = go(remote(
            x_block.at[number(block)], x_block.at[number(target)], (p, device)))

    forward((0, 0, 0), "first")
    forward((0, 0, 0), "second")

    def unrouted(slot_row):
        free = jnp.where(slot_row < 0, 1.0, 0.0)
        before = jnp.where(
            iota((tokens, tokens), 0) < iota((tokens, tokens), 1), 1.0, 0.0).astype(BF16)
        wide = jnp.broadcast_to(free, (8, tokens)).astype(BF16)
        rank = jnp.dot(wide, before, preferred_element_type=F32)[0:1]
        return jnp.where(slot_row < 0, rank, -1.0)

    spare = early.shape[2]
    load_full.wait()
    z_early = []
    z_meta = []
    for w, direction in enumerate((g, 1 - g)):
        rank = unrouted(meta[0, pl.ds(direction, 1), 0:tokens])
        chosen = jnp.where(iota((spare, tokens), 0) == rank, 1.0, 0.0).astype(BF16)
        values = jnp.dot(chosen, grad_full[direction], preferred_element_type=F32).astype(BF16)
        early[w, 0] = values[:, :half]
        early[w, 1] = values[:, half:]
        z_meta.append(remote(meta.at[0], meta.at[2 + w], (z_to[w], e)))
        z_early.append(remote(
            early.at[w], landed.at[w, :, pl.ds(landed.shape[2] - spare, spare)], (z_to[w], e)))

        @pl.when(valid(z_to[w]))
        def _():
            z_meta[w].start()
            z_early[w].start()

    load_out.wait()
    got_out.wait_recv()
    hid_base = counter[0]
    counter[0] += len(BLOCKS)

    def swap(i, there):
        return pltpu.make_async_remote_copy(
            src_ref=hid_send.at[i], dst_ref=hid_recv.at[there],
            send_sem=send_sem.at[hid_base + i], recv_sem=recv_sem.at[hid_base + there],
            device_id=(p, sibling), device_id_type=MESH)

    def hidden(block):
        i = number(block)
        w_out = w_out_chip[...].reshape(-1, half)
        hid_send[i] = lax.dot_general(
            x_block[i], w_out, (((1,), (1,)), ((), ())), preferred_element_type=F32)
        there = number((block[0], block[2], block[1]))
        pending.append(swap(i, there))
        pending[-1].start()

    def finish(block):
        i = number(block)
        c, f, s = block
        dx = f + core * (s - f)
        dy = s + core * (f - s)
        at_x = (x // 2) * 2 + (x % 2 + dx) % 2
        at_x = at_x + c * (3 - 2 * at_x)
        chip = at_x * 2 + (y + dy) % 2
        swap(i, i).wait_recv()
        total = hid_send[i] + hid_recv[i]
        parts = []
        for h in range(2):
            width = total.shape[1] // 2
            grad = total[:, h * width:(h + 1) * width]
            a = stored_chip[h, 0, chip].astype(F32)
            b = stored_chip[h, 1, chip].astype(F32)
            squashed = jax.nn.sigmoid(a)
            parts.append((grad * b * squashed * (1.0 + a * (1.0 - squashed))).astype(BF16))
            parts.append((grad * a * squashed).astype(BF16))
        pre = jnp.concatenate(parts, axis=1)
        value = jnp.dot(pre, w_in_chip[...].reshape(-1, half), preferred_element_type=F32)
        if s == 1:
            ret_send[c * 2 + f] = value.astype(BF16)
            got_ret[c, f] = go(remote(
                ret_send.at[c * 2 + f], ret_sec.at[c * 2 + f], (p, second)))
        else:
            acc[c * 2 + f] = value

    got_ret = {}
    hidden((0, 0, 0))
    got_x[0, 1, 0].wait_recv()
    forward((0, 1, 0), "second")
    hidden((0, 1, 0))
    got_x[1, 0, 0].wait_recv()
    forward((1, 0, 0), "first")
    forward((1, 0, 0), "second")
    hidden((1, 0, 0))
    load_stored.wait()
    got_stored.wait_recv()
    load_in.wait()
    got_in.wait_recv()
    finish((0, 0, 0))
    got_x[0, 0, 1].wait_recv()
    hidden((0, 0, 1))
    got_x[1, 1, 0].wait_recv()
    forward((1, 1, 0), "second")
    hidden((1, 1, 0))
    finish((0, 0, 1))
    finish((0, 1, 0))
    finish((1, 0, 0))
    got_x[0, 1, 1].wait_recv()
    hidden((0, 1, 1))
    got_x[1, 0, 1].wait_recv()
    hidden((1, 0, 1))
    finish((0, 1, 1))
    finish((1, 0, 1))
    got_x[1, 1, 1].wait_recv()
    hidden((1, 1, 1))
    finish((1, 1, 0))
    finish((1, 1, 1))

    got_first = {}
    for c in (0, 1):
        got_ret[c, 1].wait_recv()
        first_send[c] = (acc[c * 2 + 1] + ret_sec[c * 2 + 1].astype(F32)).astype(BF16)
        got_first[c] = go(remote(first_send.at[c], ret_first.at[c], (p, first)))

    def summed(c):
        got_ret[c, 0].wait_recv()
        part = acc[c * 2] + ret_sec[c * 2].astype(F32)
        got_first[c].wait_recv()
        return part + ret_first[c].astype(F32)

    wide = landed.shape[2] - spare
    step = rows - wide
    z_final, z_arrival = {}, {}

    def relay(w, total):
        final[w] = (raw[w].astype(F32) + total).astype(BF16)
        index = take()
        take()
        for k in range(2):
            z_final[w, k] = pltpu.make_async_remote_copy(
                src_ref=final.at[w, pl.ds(k * step, wide)],
                dst_ref=landed.at[w, core, pl.ds(0, wide)],
                send_sem=send_sem.at[index + k], recv_sem=recv_sem.at[index + core],
                device_id=(z_to[w], base + k), device_id_type=MESH)
            z_arrival[w, k] = pltpu.make_async_remote_copy(
                src_ref=final.at[w, pl.ds(k * step, wide)],
                dst_ref=landed.at[w, k, pl.ds(0, wide)],
                send_sem=send_sem.at[index + k], recv_sem=recv_sem.at[index + k],
                device_id=(z_to[w], base + k), device_id_type=MESH)

        @pl.when(valid(z_to[w]))
        def _():
            for k in range(2):
                z_final[w, k].start()

    own_total = summed(0)
    relay(0, own_total)
    cut_send[...] = summed(1).astype(BF16)
    got_cut = go(remote(cut_send, ret_cut, (p, cut)))
    got_cut.wait_recv()
    relay(1, ret_cut[...].astype(F32))

    eye = iota((tokens, tokens), 0) == iota((tokens, tokens), 1)
    stores = []
    for w, direction in enumerate((g, 1 - g)):
        @pl.when(valid(z_from[w]))
        def _():
            z_meta[w].wait_recv()
            z_early[w].wait_recv()
            slot_row = meta[2 + w, pl.ds(direction, 1), 0:tokens]
            rank_row = unrouted(slot_row)
            slot_col = jnp.sum(jnp.where(eye, slot_row, 0.0), axis=1, keepdims=True)
            rank_col = jnp.sum(jnp.where(eye, rank_row, 0.0), axis=1, keepdims=True)
            shift = (core * (capacity - step)).astype(F32)
            column = iota((tokens, wide + spare), 1)
            late = jnp.logical_and(slot_col >= 0, column == slot_col + shift)
            soon = jnp.logical_and(rank_col >= 0, column == rank_col + float(wide))
            select = jnp.where(jnp.logical_or(late, soon), 1.0, 0.0).astype(BF16)
            for k in range(2):
                z_arrival[w, k].wait_recv()
            for h in range(2):
                out_buf[w, :, h * half:(h + 1) * half] = jnp.dot(
                    select, landed[w, h], preferred_element_type=F32).astype(BF16)

        @pl.when(jnp.logical_not(valid(z_from[w])))
        def _():
            out_buf[w] = jnp.zeros_like(out_buf[w])

        stores.append(local(out_buf.at[w], out_hbm.at[direction], 5 + w))
        stores[w].start()

    for copy in pending:
        copy.wait_send()
    for w in range(2):
        @pl.when(valid(z_to[w]))
        def _():
            z_meta[w].wait_send()
            z_early[w].wait_send()
            for k in range(2):
                z_final[w, k].wait_send()
    for store in stores:
        store.wait()


COPIES = 64


def on_device(n_pipe, grad_out, route_slot, gate_weight, stored_pre, w_in, w_out):
    _, sources, capacity, _, hidden = stored_pre.shape
    _, tokens, features = grad_out.shape
    half, rows, chips = features // 2, 2 * capacity, sources // 2
    wide = -(-capacity // 16) * 16
    spare = -(-(tokens - capacity) // 16) * 16
    stored = jnp.transpose(stored_pre[0], (2, 0, 1, 3)).reshape(2, chips, rows, hidden)
    weight_in = jnp.transpose(w_in[0], (1, 0, 2))
    hbm = pl.BlockSpec(memory_space=pl.ANY)
    vmem = pl.BlockSpec(memory_space=pltpu.VMEM)
    half_rows = (rows, half)
    return pl.pallas_call(
        functools.partial(kernel, n_pipe, capacity),
        out_shape=jax.ShapeDtypeStruct(grad_out.shape, BF16),
        in_specs=[hbm, vmem, vmem, hbm, hbm, hbm],
        out_specs=hbm,
        scratch_shapes=[
            pltpu.VMEM((2, tokens, features), BF16),
            pltpu.VMEM((2, 2, tokens, half), BF16),
            pltpu.VMEM((4, 8, 2 * tokens), F32),
            pltpu.VMEM((2, hidden, half), BF16),
            pltpu.VMEM((2, 2, hidden, half), BF16),
            pltpu.VMEM((2, 2, chips, rows, hidden), BF16),
            pltpu.VMEM((2,) + half_rows, BF16),
            pltpu.VMEM(half_rows, BF16),
            pltpu.VMEM((8,) + half_rows, BF16),
            pltpu.VMEM((8, rows, 2 * hidden), F32),
            pltpu.VMEM((8, rows, 2 * hidden), F32),
            pltpu.VMEM((4,) + half_rows, F32),
            pltpu.VMEM((4,) + half_rows, BF16),
            pltpu.VMEM((4,) + half_rows, BF16),
            pltpu.VMEM((2,) + half_rows, BF16),
            pltpu.VMEM((2,) + half_rows, BF16),
            pltpu.VMEM(half_rows, BF16),
            pltpu.VMEM(half_rows, BF16),
            pltpu.VMEM((2,) + half_rows, BF16),
            pltpu.VMEM((2, 2, spare, half), BF16),
            pltpu.VMEM((2, 2, wide + spare, half), BF16),
            pltpu.VMEM((2, tokens, features), BF16),
            pltpu.SemaphoreType.DMA((8,)),
            pltpu.SemaphoreType.DMA((COPIES,)),
            pltpu.SemaphoreType.DMA((COPIES,)),
        ],
        compiler_params=pltpu.CompilerParams(
            collective_id=0, has_side_effects=True, vmem_limit_bytes=48 * 2**20),
    )(grad_out, route_slot, gate_weight, stored, weight_in, w_out[0])


def solution(mesh):
    return jax.shard_map(
        functools.partial(on_device, mesh.shape["pipe"]),
        mesh=mesh,
        in_specs=(
            P(None, ("pipe", "expert"), None),
            P(None, ("pipe", "expert")),
            P(None, ("pipe", "expert")),
            P("pipe", None, None, None, "expert"),
            P("pipe", "expert", None, None),
            P("pipe", "expert", None),
        ),
        out_specs=P(None, ("pipe", "expert"), None),
        check_vma=False,
    )
```

```python
import functools

import jax
import jax.numpy as jnp
from jax import lax
from jax.experimental import pallas as pl
from jax.experimental.pallas import tpu as pltpu
from jax.sharding import PartitionSpec as P

MESH = pl.DeviceIdType.MESH
F32, BF16 = jnp.float32, jnp.bfloat16
BLOCKS = [(c, f, s) for c in range(2) for f in range(2) for s in range(2)]


def number(block):
    return block[0] * 4 + block[1] * 2 + block[2]


def iota(shape, dim):
    return lax.broadcasted_iota(jnp.int32, shape, dim).astype(F32)


def kernel(
    n_pipe, capacity,
    grad_hbm, slot_ref, gate_ref, stored_hbm, w_in_hbm, w_out_hbm,
    out_hbm,
    grad_chip, meta, w_out_chip, w_in_raw, w_in_chip, stored_raw, stored_chip,
    raw, cross_block, x_block, hid_send, hid_recv, acc, ret_send, ret_sec,
    first_send, ret_first, cut_send, ret_cut, final, early, place, landed, landed_place, stage,
    local_sem, send_sem, recv_sem,
):
    tokens, half = grad_chip.shape[2:]
    rows, all_tokens = 2 * capacity, 2 * tokens
    pieces = [(0, (rows // 2 + 15) // 16 * 16)]
    pieces.append((pieces[0][1], rows - pieces[0][1]))
    p, e = lax.axis_index("pipe"), lax.axis_index("expert")
    core, y, x = e % 2, (e // 2) % 2, e // 4
    g = x // 2
    sibling = e + 1 - 2 * core
    x_next = e + 4 - 8 * (x % 2)
    y_next = e + 2 - 4 * y
    cut = e + 4 * (3 - 2 * x)
    first = x_next + core * (y_next - x_next)
    second = y_next + core * (x_next - y_next)
    z_to = [p - 1 + 2 * g, p + 1 - 2 * g]
    z_from = [z_to[1], z_to[0]]
    directions = [g, 1 - g]

    def valid(rank):
        return jnp.logical_and(rank >= 0, rank < n_pipe)

    counter = [0]

    def take(count=1):
        counter[0] += count
        return counter[0] - count

    def remote(src, dst, device):
        index = take()
        return pltpu.make_async_remote_copy(
            src_ref=src, dst_ref=dst, send_sem=send_sem.at[index], recv_sem=recv_sem.at[index],
            device_id=device, device_id_type=MESH,
        )

    local_counter = [0]

    def local(src, dst):
        local_counter[0] += 1
        copy = pltpu.make_async_copy(src, dst, local_sem.at[local_counter[0] - 1])
        copy.start()
        return copy

    barrier = pltpu.get_barrier_semaphore()
    for other in (sibling, first, second, cut):
        pl.semaphore_signal(barrier, inc=1, device_id=(p, other), device_id_type=MESH)
    for rank in z_to:
        @pl.when(valid(rank))
        def _():
            pl.semaphore_signal(barrier, inc=1, device_id=(rank, e), device_id_type=MESH)

    mine = pl.multiple_of(core * half, 128)
    theirs = pl.multiple_of((1 - core) * half, 128)

    load_grad = [None, None]
    for w in (1, 0):
        load_grad[w] = local(
            grad_hbm.at[directions[w], :, pl.ds(mine, half)], grad_chip.at[w, core])

    slot = slot_ref[...].astype(F32)
    gate = gate_ref[...]
    meta[0] = jnp.zeros_like(meta[0])
    meta[0, 0:2, 0:tokens] = slot
    meta[0, 0:2, tokens:all_tokens] = slot
    meta[0, 2:4, 0:tokens] = gate
    meta[0, 2:4, tokens:all_tokens] = gate

    pl.semaphore_wait(barrier, 4 + sum(valid(rank).astype(jnp.int32) for rank in z_to))

    pending = []

    def go(copy):
        copy.start()
        pending.append(copy)
        return copy

    got_meta = go(remote(meta.at[0], meta.at[1], (p, sibling)))
    got_grad = [None, None]
    for w in (1, 0):
        got_grad[w] = go(remote(
            grad_hbm.at[directions[w], :, pl.ds(theirs, half)], grad_chip.at[w, core],
            (p, sibling)))
    load_out = local(w_out_hbm.at[0, :, pl.ds(mine, half)], w_out_chip.at[core])
    load_stored = local(stored_hbm.at[0], stored_raw.at[core])
    load_in = local(w_in_hbm.at[0, :, :, pl.ds(mine, half)], w_in_raw.at[core])
    got_out = go(remote(w_out_hbm.at[0, :, pl.ds(theirs, half)], w_out_chip.at[core], (p, sibling)))
    got_stored = go(remote(stored_hbm.at[0], stored_raw.at[core], (p, sibling)))
    got_in = go(remote(
        w_in_hbm.at[0, :, :, pl.ds(theirs, half)], w_in_raw.at[core], (p, sibling)))
    got_meta.wait_recv()

    lane = lax.broadcasted_iota(jnp.int32, (1, all_tokens), 1)
    is_own = (lane // tokens) == core
    earlier = jnp.where(
        iota((all_tokens, all_tokens), 0) < iota((all_tokens, all_tokens), 1), 1.0, 0.0
    ).astype(BF16)

    def pack(w):
        row = pl.ds(directions[w], 1)
        gate_row = pl.ds(directions[w] + 2, 1)
        chip_slot = jnp.where(is_own, meta[0, row, :], meta[1, row, :])
        chip_gate = jnp.where(is_own, meta[0, gate_row, :], meta[1, gate_row, :])
        free = jnp.broadcast_to(jnp.where(chip_slot < 0, 1.0, 0.0), (8, all_tokens))
        rank = jnp.dot(free.astype(BF16), earlier, preferred_element_type=F32)[0:1]
        position = jnp.where(
            chip_slot < 0, rank + float(rows),
            chip_slot + jnp.where(lane >= tokens, float(capacity), 0.0))
        place[w] = jnp.broadcast_to(position, place.shape[1:])
        onehot = jnp.where(iota((all_tokens, all_tokens), 0) == position, 1.0, 0.0)
        slot_gate = jnp.sum(onehot[:rows] * chip_gate, axis=1, keepdims=True)
        load_grad[w].wait()
        got_grad[w].wait_recv()
        both = jnp.concatenate([grad_chip[w, 0], grad_chip[w, 1]], axis=0)
        picked = jnp.dot(onehot.astype(BF16), both, preferred_element_type=F32)
        raw[w] = picked[:rows].astype(BF16)
        early[w] = picked[rows:].astype(BF16)
        return (slot_gate * picked[:rows]).astype(BF16)

    cross_block[...] = pack(1)
    got_x = {}
    got_x[1, 0, 0] = go(remote(cross_block, x_block.at[number((1, 0, 0))], (p, cut)))
    x_block[0] = pack(0)

    def forward(block, along):
        c, f, s = block
        target = (c, 1, s) if along == "first" else (c, f, 1)
        device = first if along == "first" else second
        got_x[target] = go(remote(
            x_block.at[number(block)], x_block.at[number(target)], (p, device)))

    forward((0, 0, 0), "first")
    forward((0, 0, 0), "second")

    z_place = [remote(place.at[w], landed_place.at[w], (z_to[w], e)) for w in range(2)]
    z_early = [
        remote(early.at[w], landed.at[w, pl.ds(rows, all_tokens - rows)], (z_to[w], e))
        for w in range(2)]
    for w in range(2):
        @pl.when(valid(z_to[w]))
        def _():
            z_place[w].start()
            z_early[w].start()

    load_out.wait()
    got_out.wait_recv()
    hid_base = take(len(BLOCKS))

    def swap(i, there):
        return pltpu.make_async_remote_copy(
            src_ref=hid_send.at[i], dst_ref=hid_recv.at[there],
            send_sem=send_sem.at[hid_base + i], recv_sem=recv_sem.at[hid_base + there],
            device_id=(p, sibling), device_id_type=MESH)

    def hidden(block):
        i = number(block)
        w_out = w_out_chip[...].reshape(-1, half)
        hid_send[i] = lax.dot_general(
            x_block[i], w_out, (((1,), (1,)), ((), ())), preferred_element_type=F32)
        pending.append(swap(i, number((block[0], block[2], block[1]))))
        pending[-1].start()

    def finish(block):
        i = number(block)
        c, f, s = block
        dx = f + core * (s - f)
        dy = s + core * (f - s)
        at_x = (x // 2) * 2 + (x % 2 + dx) % 2
        at_x = at_x + c * (3 - 2 * at_x)
        chip = at_x * 2 + (y + dy) % 2
        chip_rows = pl.ds(pl.multiple_of(chip * rows, 16), rows)
        swap(i, i).wait_recv()
        total = hid_send[i] + hid_recv[i]
        parts = []
        for h in range(2):
            width = total.shape[1] // 2
            grad = total[:, h * width:(h + 1) * width]
            a = stored_chip[h, 0, chip_rows, :].astype(F32)
            b = stored_chip[h, 1, chip_rows, :].astype(F32)
            squashed = jax.nn.sigmoid(a)
            parts.append((grad * b * squashed * (1.0 + a * (1.0 - squashed))).astype(BF16))
            parts.append((grad * a * squashed).astype(BF16))
        pre = jnp.concatenate(parts, axis=1)
        value = jnp.dot(pre, w_in_chip[...].reshape(-1, half), preferred_element_type=F32)
        if s == 1:
            ret_send[c * 2 + f] = value.astype(BF16)
        else:
            acc[c * 2 + f] = value

    def in_pieces(src, dst, other):
        return [go(remote(src.at[pl.ds(*piece)], dst.at[pl.ds(*piece)], (p, other)))
                for piece in pieces]

    got_ret, got_first = {}, {}

    def send_second(c, f):
        got_ret[c, f] = in_pieces(ret_send.at[c * 2 + f], ret_sec.at[c * 2 + f], second)

    def send_first(c):
        got_first[c] = []
        for k, (start, count) in enumerate(pieces):
            span = pl.ds(start, count)
            got_ret[c, 1][k].wait_recv()
            first_send[c, span] = (
                acc[c * 2 + 1, span] + ret_sec[c * 2 + 1, span].astype(F32)).astype(BF16)
            got_first[c].append(go(remote(
                first_send.at[c, span], ret_first.at[c, span], (p, first))))

    def summed(c, k):
        span = pl.ds(*pieces[k])
        got_ret[c, 0][k].wait_recv()
        part = acc[c * 2, span] + ret_sec[c * 2, span].astype(F32)
        got_first[c][k].wait_recv()
        return part + ret_first[c, span].astype(F32)

    def arrive(block):
        got_x[block].wait_recv()
        hidden(block)

    hidden((0, 0, 0))
    load_stored.wait()
    got_stored.wait_recv()
    load_in.wait()
    got_in.wait_recv()
    for h in range(2):
        hidden_units = stored_chip.shape[3]
        stored_chip[h] = jnp.transpose(
            stored_raw[h].reshape(-1, 2, hidden_units), (1, 0, 2))
        w_in_chip[h] = jnp.transpose(w_in_raw[h], (1, 0, 2))
    got_x[1, 0, 0].wait_recv()
    forward((1, 0, 0), "first")
    forward((1, 0, 0), "second")
    hidden((1, 0, 0))
    arrive((0, 1, 0))
    arrive((0, 0, 1))
    finish((0, 0, 0))
    finish((1, 0, 0))
    got_x[1, 1, 0].wait_recv()
    forward((1, 1, 0), "second")
    forward((0, 1, 0), "second")
    hidden((1, 1, 0))
    arrive((1, 0, 1))
    finish((1, 0, 1))
    finish((1, 1, 0))
    finish((0, 1, 0))
    arrive((1, 1, 1))
    finish((1, 1, 1))
    send_second(1, 1)
    send_second(1, 0)
    finish((0, 0, 1))
    arrive((0, 1, 1))
    finish((0, 1, 1))
    send_second(0, 1)
    send_second(0, 0)

    send_first(1)
    got_cut = []
    for k, (start, count) in enumerate(pieces):
        span = pl.ds(start, count)
        cut_send[span] = summed(1, k).astype(BF16)
        got_cut.append(go(remote(cut_send.at[span], ret_cut.at[span], (p, cut))))
    send_first(0)

    z_late = [[], []]

    def relay(w, k, total):
        span = pl.ds(*pieces[k])
        final[w, span] = (raw[w, span].astype(F32) + total).astype(BF16)
        copy = remote(final.at[w, span], landed.at[w, span], (z_to[w], e))
        z_late[w].append(copy)

        @pl.when(valid(z_to[w]))
        def _():
            copy.start()

    for k in range(len(pieces)):
        got_cut[k].wait_recv()
        relay(1, k, ret_cut[pl.ds(*pieces[k])].astype(F32))
    for k in range(len(pieces)):
        relay(0, k, summed(0, k))

    eye = iota((all_tokens, all_tokens), 0) == iota((all_tokens, all_tokens), 1)
    stores = []
    for w in (1, 0):
        @pl.when(valid(z_from[w]))
        def _():
            z_place[w].wait_recv()
            z_early[w].wait_recv()
            position = jnp.sum(
                jnp.where(eye, landed_place[w, 0:1, :], 0.0), axis=1, keepdims=True)
            select = jnp.where(
                iota((all_tokens, all_tokens), 1) == position, 1.0, 0.0).astype(BF16)
            for copy in z_late[w]:
                copy.wait_recv()
            value = jnp.dot(select, landed[w], preferred_element_type=F32).astype(BF16)
            stage[w, 0] = value[:tokens]
            stage[w, 1] = value[tokens:]

        @pl.when(jnp.logical_not(valid(z_from[w])))
        def _():
            stage[w] = jnp.zeros_like(stage[w])

        target = out_hbm.at[directions[w], :, pl.ds(mine, half)]
        stores.append(go(remote(stage.at[w, 1 - core], target, (p, sibling))).wait_recv)
        stores.append(local(stage.at[w, core], target).wait)

    for wait in stores:
        wait()
    for copy in pending:
        copy.wait_send()
    for w in range(2):
        @pl.when(valid(z_to[w]))
        def _():
            for copy in [z_place[w], z_early[w]] + z_late[w]:
                copy.wait_send()


COPIES = 64


def on_device(n_pipe, grad_out, route_slot, gate_weight, stored_pre, w_in, w_out):
    _, sources, capacity, _, hidden = stored_pre.shape
    _, tokens, features = grad_out.shape
    half, rows, chips = features // 2, 2 * capacity, sources // 2
    hbm = pl.BlockSpec(memory_space=pltpu.HBM)
    vmem = pl.BlockSpec(memory_space=pltpu.VMEM)
    half_rows = (rows, half)
    return pl.pallas_call(
        functools.partial(kernel, n_pipe, capacity),
        out_shape=jax.ShapeDtypeStruct(grad_out.shape, BF16),
        in_specs=[hbm, vmem, vmem, hbm, hbm, hbm],
        out_specs=hbm,
        scratch_shapes=[
            pltpu.VMEM((2, 2, tokens, half), BF16),
            pltpu.VMEM((2, 8, 2 * tokens), F32),
            pltpu.VMEM((2, hidden, half), BF16),
            pltpu.VMEM((2, hidden, 2, half), BF16),
            pltpu.VMEM((2, 2, hidden, half), BF16),
            pltpu.VMEM((2, sources, capacity, 2, hidden), BF16),
            pltpu.VMEM((2, 2, sources * capacity, hidden), BF16),
            pltpu.VMEM((2,) + half_rows, BF16),
            pltpu.VMEM(half_rows, BF16),
            pltpu.VMEM((8,) + half_rows, BF16),
            pltpu.VMEM((8, rows, 2 * hidden), F32),
            pltpu.VMEM((8, rows, 2 * hidden), F32),
            pltpu.VMEM((4,) + half_rows, F32),
            pltpu.VMEM((4,) + half_rows, BF16),
            pltpu.VMEM((4,) + half_rows, BF16),
            pltpu.VMEM((2,) + half_rows, BF16),
            pltpu.VMEM((2,) + half_rows, BF16),
            pltpu.VMEM(half_rows, BF16),
            pltpu.VMEM(half_rows, BF16),
            pltpu.VMEM((2,) + half_rows, BF16),
            pltpu.VMEM((2, 2 * tokens - rows, half), BF16),
            pltpu.VMEM((2, 8, 2 * tokens), F32),
            pltpu.VMEM((2, 2 * tokens, half), BF16),
            pltpu.VMEM((2, 8, 2 * tokens), F32),
            pltpu.VMEM((2, 2, tokens, half), BF16),
            pltpu.SemaphoreType.DMA((8,)),
            pltpu.SemaphoreType.DMA((COPIES,)),
            pltpu.SemaphoreType.DMA((COPIES,)),
        ],
        compiler_params=pltpu.CompilerParams(
            collective_id=0, has_side_effects=True, vmem_limit_bytes=62 * 2**20),
    )(grad_out, route_slot, gate_weight, stored_pre, w_in, w_out)


def solution(mesh):
    return jax.shard_map(
        functools.partial(on_device, mesh.shape["pipe"]),
        mesh=mesh,
        in_specs=(
            P(None, ("pipe", "expert"), None),
            P(None, ("pipe", "expert")),
            P(None, ("pipe", "expert")),
            P("pipe", None, None, None, "expert"),
            P("pipe", "expert", None, None),
            P("pipe", "expert", None),
        ),
        out_specs=P(None, ("pipe", "expert"), None),
        check_vma=False,
    )
```

```python
import functools

import jax
import jax.numpy as jnp
from jax import lax
from jax.experimental import pallas as pl
from jax.experimental.pallas import tpu as pltpu
from jax.sharding import PartitionSpec as P

MESH = pl.DeviceIdType.MESH
F32, BF16 = jnp.float32, jnp.bfloat16
BLOCKS = [(c, f, s) for c in range(2) for f in range(2) for s in range(2)]


OUT_ROWS, BACK_ROWS = 16, 16
COPIES = 200


def row_pieces(rows, most):
    return [(start, min(most, rows - start)) for start in range(0, rows, most)]


def number(block):
    return block[0] * 4 + block[1] * 2 + block[2]


def iota(shape, dim):
    return lax.broadcasted_iota(jnp.int32, shape, dim).astype(F32)


def kernel(
    n_pipe, capacity,
    grad_hbm, slot_ref, gate_ref, stored_hbm, w_in_hbm, w_out_hbm,
    out_hbm,
    grad_chip, meta, w_out_chip, w_in_raw, w_in_chip, stored_raw, stored_chip,
    cross_block, x_block, cross_gate, x_gate, hid_send, hid_recv, acc, ret_send, ret_sec,
    first_send, ret_first, final, ret_cut, early, place, landed, landed_place, stage,
    local_sem, send_sem, recv_sem,
):
    tokens, half = grad_chip.shape[2:]
    rows, all_tokens = 2 * capacity, 2 * tokens
    out_pieces, pieces = row_pieces(rows, OUT_ROWS), row_pieces(rows, BACK_ROWS)
    p, e = lax.axis_index("pipe"), lax.axis_index("expert")
    core, y, x = e % 2, (e // 2) % 2, e // 4
    g = x // 2
    sibling = e + 1 - 2 * core
    x_next = e + 4 - 8 * (x % 2)
    y_next = e + 2 - 4 * y
    cut = e + 4 * (3 - 2 * x)
    first = x_next + core * (y_next - x_next)
    second = y_next + core * (x_next - y_next)
    z_to = [p - 1 + 2 * g, p + 1 - 2 * g]
    z_from = [z_to[1], z_to[0]]
    directions = [g, 1 - g]

    def valid(rank):
        return jnp.logical_and(rank >= 0, rank < n_pipe)

    counter = [0]

    def take(count=1):
        counter[0] += count
        return counter[0] - count

    def remote(src, dst, device):
        index = take()
        return pltpu.make_async_remote_copy(
            src_ref=src, dst_ref=dst, send_sem=send_sem.at[index], recv_sem=recv_sem.at[index],
            device_id=device, device_id_type=MESH,
        )

    local_counter = [0]

    def local(src, dst):
        local_counter[0] += 1
        copy = pltpu.make_async_copy(src, dst, local_sem.at[local_counter[0] - 1])
        copy.start()
        return copy

    def far(rank):
        ring = n_pipe // 2
        return jnp.logical_and(valid(rank), rank // ring != p // ring)

    is_far = [far(rank).astype(jnp.int32) for rank in z_to]
    late_to = [e + flag * (y_next - e) for flag in is_far]
    turn_first, turn_second = is_far[0] * core, is_far[0] * (1 - core)

    barrier = pltpu.get_barrier_semaphore()
    for other in (sibling, first, second, cut):
        pl.semaphore_signal(barrier, inc=1, device_id=(p, other), device_id_type=MESH)
    for rank in z_to:
        @pl.when(valid(rank))
        def _():
            pl.semaphore_signal(barrier, inc=1, device_id=(rank, e), device_id_type=MESH)

        @pl.when(far(rank))
        def _():
            pl.semaphore_signal(barrier, inc=1, device_id=(rank, y_next), device_id_type=MESH)

    mine = pl.multiple_of(core * half, 128)
    theirs = pl.multiple_of((1 - core) * half, 128)

    load_grad = [None, None]
    for w in (1, 0):
        load_grad[w] = local(
            grad_hbm.at[directions[w], :, pl.ds(mine, half)], grad_chip.at[w, core])

    slot = slot_ref[...].astype(F32)
    gate = gate_ref[...]
    meta[0] = jnp.zeros_like(meta[0])
    meta[0, 0:2, 0:tokens] = slot
    meta[0, 0:2, tokens:all_tokens] = slot
    meta[0, 2:4, 0:tokens] = gate
    meta[0, 2:4, tokens:all_tokens] = gate

    pl.semaphore_wait(
        barrier, 4 + sum(valid(rank).astype(jnp.int32) for rank in z_to) + sum(is_far))

    pending = []

    def go(copy):
        copy.start()
        pending.append(copy)
        return copy

    def in_pieces(spans, src, dst, other):
        return [go(remote(src.at[pl.ds(*span)], dst.at[pl.ds(*span)], (p, other)))
                for span in spans]

    got_meta = go(remote(meta.at[0], meta.at[1], (p, sibling)))
    got_grad = [None, None]
    for w in (1, 0):
        got_grad[w] = go(remote(
            grad_hbm.at[directions[w], :, pl.ds(theirs, half)], grad_chip.at[w, core],
            (p, sibling)))
    load_out = local(w_out_hbm.at[0, :, pl.ds(mine, half)], w_out_chip.at[core])
    load_stored = local(stored_hbm.at[0], stored_raw.at[core])
    load_in = local(w_in_hbm.at[0, :, :, pl.ds(mine, half)], w_in_raw.at[core])
    got_out = go(remote(w_out_hbm.at[0, :, pl.ds(theirs, half)], w_out_chip.at[core], (p, sibling)))
    got_stored = go(remote(stored_hbm.at[0], stored_raw.at[core], (p, sibling)))
    got_in = go(remote(
        w_in_hbm.at[0, :, :, pl.ds(theirs, half)], w_in_raw.at[core], (p, sibling)))
    got_meta.wait_recv()

    lane = lax.broadcasted_iota(jnp.int32, (1, all_tokens), 1)
    is_own = (lane // tokens) == core
    earlier = jnp.where(
        iota((all_tokens, all_tokens), 0) < iota((all_tokens, all_tokens), 1), 1.0, 0.0
    ).astype(BF16)

    slot_eye = iota((rows, all_tokens), 0) == iota((rows, all_tokens), 1)

    def pack(w):
        row = pl.ds(directions[w], 1)
        gate_row = pl.ds(directions[w] + 2, 1)
        chip_slot = jnp.where(is_own, meta[0, row, :], meta[1, row, :])
        chip_gate = jnp.where(is_own, meta[0, gate_row, :], meta[1, gate_row, :])
        free = jnp.broadcast_to(jnp.where(chip_slot < 0, 1.0, 0.0), (8, all_tokens))
        rank = jnp.dot(free.astype(BF16), earlier, preferred_element_type=F32)[0:1]
        position = jnp.where(
            chip_slot < 0, rank + float(rows),
            chip_slot + jnp.where(lane >= tokens, float(capacity), 0.0))
        place[w] = jnp.broadcast_to(position, place.shape[1:])
        onehot = jnp.where(iota((all_tokens, all_tokens), 0) == position, 1.0, 0.0)
        slot_gate = jnp.sum(onehot[:rows] * chip_gate, axis=1, keepdims=True)
        load_grad[w].wait()
        got_grad[w].wait_recv()
        both = jnp.concatenate([grad_chip[w, 0], grad_chip[w, 1]], axis=0)
        picked = jnp.dot(onehot.astype(BF16), both, preferred_element_type=F32)
        early[w] = picked[rows:].astype(BF16)
        gates = jnp.sum(jnp.where(slot_eye, slot_gate, 0.0), axis=0, keepdims=True)
        return picked[:rows].astype(BF16), jnp.broadcast_to(gates, cross_gate.shape)

    cross_block[...], cross_gate[...] = pack(1)
    got_x = {}
    got_x[1, 0, 0] = in_pieces(out_pieces, cross_block, x_block.at[number((1, 0, 0))], cut)
    got_gate = {(1, 0, 0): go(remote(cross_gate, x_gate.at[number((1, 0, 0))], (p, cut)))}
    x_block[0], x_gate[0] = pack(0)

    def forward(block, *axes):
        c, f, s = block
        targets = {"first": (c, 1, s), "second": (c, f, 1)}
        for axis in axes:
            got_x[targets[axis]] = []
        for k, (start, count) in enumerate(out_pieces):
            span = pl.ds(start, count)
            if block in got_x and block not in arrived:
                got_x[block][k].wait_recv()
            for axis in axes:
                got_x[targets[axis]].append(go(remote(
                    x_block.at[number(block), span], x_block.at[number(targets[axis]), span],
                    (p, first if axis == "first" else second))))
        if block in got_gate and block not in arrived:
            got_gate[block].wait_recv()
        for axis in axes:
            got_gate[targets[axis]] = go(remote(
                x_gate.at[number(block)], x_gate.at[number(targets[axis])],
                (p, first if axis == "first" else second)))
        arrived.add(block)

    arrived = set()
    forward((0, 0, 0), "first", "second")

    z_place = [remote(place.at[w], landed_place.at[w], (z_to[w], e)) for w in range(2)]
    z_early = [
        remote(early.at[w], landed.at[w, pl.ds(rows, all_tokens - rows)], (z_to[w], e))
        for w in range(2)]
    for w in range(2):
        @pl.when(valid(z_to[w]))
        def _():
            z_place[w].start()
            z_early[w].start()

    load_out.wait()
    got_out.wait_recv()
    hid_base = take(len(BLOCKS))

    def swap(i, there):
        return pltpu.make_async_remote_copy(
            src_ref=hid_send.at[i], dst_ref=hid_recv.at[there],
            send_sem=send_sem.at[hid_base + i], recv_sem=recv_sem.at[hid_base + there],
            device_id=(p, sibling), device_id_type=MESH)

    def hidden(block):
        i = number(block)
        w_out = w_out_chip[...].reshape(-1, half)
        hid_send[i] = lax.dot_general(
            x_block[i], w_out, (((1,), (1,)), ((), ())), preferred_element_type=F32)
        pending.append(swap(i, number((block[0], block[2], block[1]))))
        pending[-1].start()

    def finish(block):
        i = number(block)
        c, f, s = block
        dx = f + core * (s - f)
        dy = s + core * (f - s)
        at_x = (x // 2) * 2 + (x % 2 + dx) % 2
        at_x = at_x + c * (3 - 2 * at_x)
        chip = at_x * 2 + (y + dy) % 2
        chip_rows = pl.ds(pl.multiple_of(chip * rows, 16), rows)
        swap(i, i).wait_recv()
        slot_gate = jnp.sum(jnp.where(slot_eye, x_gate[i, 0:1, :], 0.0), axis=1, keepdims=True)
        total = (hid_send[i] + hid_recv[i]) * slot_gate
        parts = []
        for h in range(2):
            width = total.shape[1] // 2
            grad = total[:, h * width:(h + 1) * width]
            a = stored_chip[h, 0, chip_rows, :].astype(F32)
            b = stored_chip[h, 1, chip_rows, :].astype(F32)
            squashed = jax.nn.sigmoid(a)
            parts.append((grad * b * squashed * (1.0 + a * (1.0 - squashed))).astype(BF16))
            parts.append((grad * a * squashed).astype(BF16))
        pre = jnp.concatenate(parts, axis=1)
        value = jnp.dot(pre, w_in_chip[...].reshape(-1, half), preferred_element_type=F32)
        acc[i] = value

    def block_of(c, f, s):
        flip = lambda bit, turn: 1 - turn if bit else turn
        return c * 4 + flip(f, turn_first) * 2 + flip(s, turn_second)

    got_ret, got_first = {}, {}

    def send_second(c, f):
        ret_send[c * 2 + f] = acc[block_of(c, f, 1)].astype(BF16)
        got_ret[c, f] = in_pieces(
            pieces, ret_send.at[c * 2 + f], ret_sec.at[c * 2 + f], second)

    def send_first(c):
        got_first[c] = []
        for k, (start, count) in enumerate(pieces):
            span = pl.ds(start, count)
            got_ret[c, 1][k].wait_recv()
            first_send[c, span] = (
                acc[block_of(c, 1, 0), span] + ret_sec[c * 2 + 1, span].astype(F32)).astype(BF16)
            got_first[c].append(go(remote(
                first_send.at[c, span], ret_first.at[c, span], (p, first))))

    def summed(c, k):
        span = pl.ds(*pieces[k])
        got_ret[c, 0][k].wait_recv()
        i = block_of(c, 0, 0)
        part = acc[i, span] + ret_sec[c * 2, span].astype(F32)
        got_first[c][k].wait_recv()
        total = part + ret_first[c, span].astype(F32)
        final[c, span] = (x_block[i, span].astype(F32) + total).astype(BF16)
        return final.at[c, span]

    def arrive(block):
        if block not in arrived:
            for copy in got_x[block]:
                copy.wait_recv()
            got_gate[block].wait_recv()
            arrived.add(block)
        hidden(block)

    hidden((0, 0, 0))
    load_stored.wait()
    got_stored.wait_recv()
    load_in.wait()
    got_in.wait_recv()
    for h in range(2):
        hidden_units = stored_chip.shape[3]
        stored_chip[h] = jnp.transpose(
            stored_raw[h].reshape(-1, 2, hidden_units), (1, 0, 2))
        w_in_chip[h] = jnp.transpose(w_in_raw[h], (1, 0, 2))
    forward((1, 0, 0), "first", "second")
    hidden((1, 0, 0))
    arrive((0, 1, 0))
    arrive((0, 0, 1))
    finish((0, 0, 0))
    finish((1, 0, 0))
    forward((1, 1, 0), "second")
    forward((0, 1, 0), "second")
    hidden((1, 1, 0))
    arrive((1, 0, 1))
    finish((1, 0, 1))
    finish((1, 1, 0))
    finish((0, 1, 0))
    arrive((1, 1, 1))
    finish((1, 1, 1))
    send_second(1, 1)
    send_second(1, 0)
    finish((0, 0, 1))
    arrive((0, 1, 1))
    finish((0, 1, 1))
    send_second(0, 1)
    send_second(0, 0)

    send_first(1)
    got_cut = []
    for k, (start, count) in enumerate(pieces):
        got_cut.append(go(remote(summed(1, k), ret_cut.at[pl.ds(start, count)], (p, cut))))
    send_first(0)

    z_late = [[], []]

    def relay(w, k, rows_ref):
        copy = remote(rows_ref, landed.at[w, pl.ds(*pieces[k])], (z_to[w], late_to[w]))
        z_late[w].append(copy)

        @pl.when(valid(z_to[w]))
        def _():
            copy.start()

    for k in range(len(pieces)):
        got_cut[k].wait_recv()
        relay(1, k, ret_cut.at[pl.ds(*pieces[k])])
    for k in range(len(pieces)):
        relay(0, k, summed(0, k))

    eye = iota((all_tokens, all_tokens), 0) == iota((all_tokens, all_tokens), 1)
    stores = []
    for w in (1, 0):
        @pl.when(valid(z_from[w]))
        def _():
            z_place[w].wait_recv()
            z_early[w].wait_recv()
            position = jnp.sum(
                jnp.where(eye, landed_place[w, 0:1, :], 0.0), axis=1, keepdims=True)
            select = jnp.where(
                iota((all_tokens, all_tokens), 1) == position, 1.0, 0.0).astype(BF16)
            for copy in z_late[w]:
                copy.wait_recv()
            value = jnp.dot(select, landed[w], preferred_element_type=F32).astype(BF16)
            stage[w, 0] = value[:tokens]
            stage[w, 1] = value[tokens:]

        @pl.when(jnp.logical_not(valid(z_from[w])))
        def _():
            stage[w] = jnp.zeros_like(stage[w])

        target = out_hbm.at[directions[w], :, pl.ds(mine, half)]
        stores.append(go(remote(stage.at[w, 1 - core], target, (p, sibling))).wait_recv)
        stores.append(local(stage.at[w, core], target).wait)

    for wait in stores:
        wait()
    for copy in pending:
        copy.wait_send()
    for w in range(2):
        @pl.when(valid(z_to[w]))
        def _():
            for copy in [z_place[w], z_early[w]] + z_late[w]:
                copy.wait_send()


def on_device(n_pipe, grad_out, route_slot, gate_weight, stored_pre, w_in, w_out):
    _, sources, capacity, _, hidden = stored_pre.shape
    _, tokens, features = grad_out.shape
    half, rows, chips = features // 2, 2 * capacity, sources // 2
    hbm = pl.BlockSpec(memory_space=pltpu.HBM)
    vmem = pl.BlockSpec(memory_space=pltpu.VMEM)
    half_rows = (rows, half)
    return pl.pallas_call(
        functools.partial(kernel, n_pipe, capacity),
        out_shape=jax.ShapeDtypeStruct(grad_out.shape, BF16),
        in_specs=[hbm, vmem, vmem, hbm, hbm, hbm],
        out_specs=hbm,
        scratch_shapes=[
            pltpu.VMEM((2, 2, tokens, half), BF16),
            pltpu.VMEM((2, 8, 2 * tokens), F32),
            pltpu.VMEM((2, hidden, half), BF16),
            pltpu.VMEM((2, hidden, 2, half), BF16),
            pltpu.VMEM((2, 2, hidden, half), BF16),
            pltpu.VMEM((2, sources, capacity, 2, hidden), BF16),
            pltpu.VMEM((2, 2, sources * capacity, hidden), BF16),
            pltpu.VMEM(half_rows, BF16),
            pltpu.VMEM((8,) + half_rows, BF16),
            pltpu.VMEM((8, 2 * tokens), F32),
            pltpu.VMEM((8, 8, 2 * tokens), F32),
            pltpu.VMEM((8, rows, 2 * hidden), F32),
            pltpu.VMEM((8, rows, 2 * hidden), F32),
            pltpu.VMEM((8,) + half_rows, F32),
            pltpu.VMEM((4,) + half_rows, BF16),
            pltpu.VMEM((4,) + half_rows, BF16),
            pltpu.VMEM((2,) + half_rows, BF16),
            pltpu.VMEM((2,) + half_rows, BF16),
            pltpu.VMEM((2,) + half_rows, BF16),
            pltpu.VMEM(half_rows, BF16),
            pltpu.VMEM((2, 2 * tokens - rows, half), BF16),
            pltpu.VMEM((2, 8, 2 * tokens), F32),
            pltpu.VMEM((2, 2 * tokens, half), BF16),
            pltpu.VMEM((2, 8, 2 * tokens), F32),
            pltpu.VMEM((2, 2, tokens, half), BF16),
            pltpu.SemaphoreType.DMA((8,)),
            pltpu.SemaphoreType.DMA((COPIES,)),
            pltpu.SemaphoreType.DMA((COPIES,)),
        ],
        compiler_params=pltpu.CompilerParams(
            collective_id=0, has_side_effects=True, vmem_limit_bytes=62 * 2**20),
    )(grad_out, route_slot, gate_weight, stored_pre, w_in, w_out)


def solution(mesh):
    return jax.shard_map(
        functools.partial(on_device, mesh.shape["pipe"]),
        mesh=mesh,
        in_specs=(
            P(None, ("pipe", "expert"), None),
            P(None, ("pipe", "expert")),
            P(None, ("pipe", "expert")),
            P("pipe", None, None, None, "expert"),
            P("pipe", "expert", None, None),
            P("pipe", "expert", None),
        ),
        out_specs=P(None, ("pipe", "expert"), None),
        check_vma=False,
    )
```

```python
import functools

import jax
import jax.numpy as jnp
from jax import lax
from jax.experimental import pallas as pl
from jax.experimental.pallas import tpu as pltpu
from jax.sharding import PartitionSpec as P

MESH = pl.DeviceIdType.MESH
F32, BF16 = jnp.float32, jnp.bfloat16
BLOCKS = [(c, f, s) for c in range(2) for f in range(2) for s in range(2)]


OUT_ROWS, BACK_ROWS = 16, 16
COPIES = 200


def row_pieces(rows, most):
    return [(start, min(most, rows - start)) for start in range(0, rows, most)]


def number(block):
    return block[0] * 4 + block[1] * 2 + block[2]


def iota(shape, dim):
    return lax.broadcasted_iota(jnp.int32, shape, dim).astype(F32)


def kernel(
    n_pipe, capacity,
    grad_hbm, slot_ref, gate_ref, stored_hbm, w_in_hbm, w_out_hbm,
    out_hbm,
    grad_chip, meta, w_out_chip, w_in_raw, w_in_chip, stored_raw, stored_chip,
    cross_block, x_block, cross_gate, x_gate, hid_send, hid_recv, acc, ret_send, ret_sec,
    first_send, ret_first, final, ret_cut, early, place, landed, landed_place, stage,
    local_sem, send_sem, recv_sem,
):
    tokens, half = grad_chip.shape[2:]
    rows, all_tokens = 2 * capacity, 2 * tokens
    out_pieces, pieces = row_pieces(rows, OUT_ROWS), row_pieces(rows, BACK_ROWS)
    p, e = lax.axis_index("pipe"), lax.axis_index("expert")
    core, y, x = e % 2, (e // 2) % 2, e // 4
    g = x // 2
    sibling = e + 1 - 2 * core
    x_next = e + 4 - 8 * (x % 2)
    y_next = e + 2 - 4 * y
    cut = e + 4 * (3 - 2 * x)
    first = x_next + core * (y_next - x_next)
    second = y_next + core * (x_next - y_next)
    z_to = [p - 1 + 2 * g, p + 1 - 2 * g]
    z_from = [z_to[1], z_to[0]]
    directions = [g, 1 - g]

    def valid(rank):
        return jnp.logical_and(rank >= 0, rank < n_pipe)

    counter = [0]

    def take(count=1):
        counter[0] += count
        return counter[0] - count

    def remote(src, dst, device):
        index = take()
        return pltpu.make_async_remote_copy(
            src_ref=src, dst_ref=dst, send_sem=send_sem.at[index], recv_sem=recv_sem.at[index],
            device_id=device, device_id_type=MESH,
        )

    local_counter = [0]

    def local(src, dst):
        local_counter[0] += 1
        copy = pltpu.make_async_copy(src, dst, local_sem.at[local_counter[0] - 1])
        copy.start()
        return copy

    def far(rank):
        ring = n_pipe // 2
        return jnp.logical_and(valid(rank), rank // ring != p // ring)

    is_far = [far(rank).astype(jnp.int32) for rank in z_to]
    late_to = [e + flag * (y_next - e) for flag in is_far]
    turn_first, turn_second = is_far[0] * core, is_far[0] * (1 - core)

    barrier = pltpu.get_barrier_semaphore()
    for other in (sibling, first, second, cut):
        pl.semaphore_signal(barrier, inc=1, device_id=(p, other), device_id_type=MESH)
    for rank in z_to:
        @pl.when(valid(rank))
        def _():
            pl.semaphore_signal(barrier, inc=1, device_id=(rank, e), device_id_type=MESH)

        @pl.when(far(rank))
        def _():
            pl.semaphore_signal(barrier, inc=1, device_id=(rank, y_next), device_id_type=MESH)

    mine = pl.multiple_of(core * half, 128)
    theirs = pl.multiple_of((1 - core) * half, 128)

    load_grad = [None, None]
    for w in (0, 1):
        load_grad[w] = local(
            grad_hbm.at[directions[w], :, pl.ds(mine, half)], grad_chip.at[w, core])

    slot = slot_ref[...].astype(F32)
    gate = gate_ref[...]
    meta[0] = jnp.zeros_like(meta[0])
    meta[0, 0:2, 0:tokens] = slot
    meta[0, 0:2, tokens:all_tokens] = slot
    meta[0, 2:4, 0:tokens] = gate
    meta[0, 2:4, tokens:all_tokens] = gate

    pl.semaphore_wait(
        barrier, 4 + sum(valid(rank).astype(jnp.int32) for rank in z_to) + sum(is_far))

    pending = []

    def go(copy):
        copy.start()
        pending.append(copy)
        return copy

    def in_pieces(spans, src, dst, other):
        return [go(remote(src.at[pl.ds(*span)], dst.at[pl.ds(*span)], (p, other)))
                for span in spans]

    got_meta = go(remote(meta.at[0], meta.at[1], (p, sibling)))
    got_grad = [None, None]
    for w in (0, 1):
        got_grad[w] = go(remote(
            grad_hbm.at[directions[w], :, pl.ds(theirs, half)], grad_chip.at[w, core],
            (p, sibling)))
    got_meta.wait_recv()

    lane = lax.broadcasted_iota(jnp.int32, (1, all_tokens), 1)
    is_own = (lane // tokens) == core
    earlier = jnp.where(
        iota((all_tokens, all_tokens), 0) < iota((all_tokens, all_tokens), 1), 1.0, 0.0
    ).astype(BF16)

    slot_eye = iota((rows, all_tokens), 0) == iota((rows, all_tokens), 1)

    def pack(w):
        row = pl.ds(directions[w], 1)
        gate_row = pl.ds(directions[w] + 2, 1)
        chip_slot = jnp.where(is_own, meta[0, row, :], meta[1, row, :])
        chip_gate = jnp.where(is_own, meta[0, gate_row, :], meta[1, gate_row, :])
        free = jnp.broadcast_to(jnp.where(chip_slot < 0, 1.0, 0.0), (8, all_tokens))
        rank = jnp.dot(free.astype(BF16), earlier, preferred_element_type=F32)[0:1]
        position = jnp.where(
            chip_slot < 0, rank + float(rows),
            chip_slot + jnp.where(lane >= tokens, float(capacity), 0.0))
        place[w] = jnp.broadcast_to(position, place.shape[1:])
        onehot = jnp.where(iota((all_tokens, all_tokens), 0) == position, 1.0, 0.0)
        slot_gate = jnp.sum(onehot[:rows] * chip_gate, axis=1, keepdims=True)
        load_grad[w].wait()
        got_grad[w].wait_recv()
        both = jnp.concatenate([grad_chip[w, 0], grad_chip[w, 1]], axis=0)
        picked = jnp.dot(onehot.astype(BF16), both, preferred_element_type=F32)
        early[w] = picked[rows:].astype(BF16)
        gates = jnp.sum(jnp.where(slot_eye, slot_gate, 0.0), axis=0, keepdims=True)
        return picked[:rows].astype(BF16), jnp.broadcast_to(gates, cross_gate.shape)

    got_x, got_gate, arrived = {}, {}, set()

    def forward(block, *axes):
        c, f, s = block
        targets = {"first": (c, 1, s), "second": (c, f, 1)}
        for axis in axes:
            got_x[targets[axis]] = []
        for k, (start, count) in enumerate(out_pieces):
            span = pl.ds(start, count)
            if block in got_x and block not in arrived:
                got_x[block][k].wait_recv()
            for axis in axes:
                got_x[targets[axis]].append(go(remote(
                    x_block.at[number(block), span], x_block.at[number(targets[axis]), span],
                    (p, first if axis == "first" else second))))
        if block in got_gate and block not in arrived:
            got_gate[block].wait_recv()
        for axis in axes:
            got_gate[targets[axis]] = go(remote(
                x_gate.at[number(block)], x_gate.at[number(targets[axis])],
                (p, first if axis == "first" else second)))
        arrived.add(block)

    x_block[0], x_gate[0] = pack(0)
    forward((0, 0, 0), "first", "second")
    cross_block[...], cross_gate[...] = pack(1)
    got_x[1, 0, 0] = in_pieces(out_pieces, cross_block, x_block.at[number((1, 0, 0))], cut)
    got_gate[1, 0, 0] = go(remote(cross_gate, x_gate.at[number((1, 0, 0))], (p, cut)))

    load_out = local(w_out_hbm.at[0, :, pl.ds(mine, half)], w_out_chip.at[core])
    load_stored = local(stored_hbm.at[0], stored_raw.at[core])
    load_in = local(w_in_hbm.at[0, :, :, pl.ds(mine, half)], w_in_raw.at[core])
    got_out = go(remote(w_out_hbm.at[0, :, pl.ds(theirs, half)], w_out_chip.at[core], (p, sibling)))
    got_stored = go(remote(stored_hbm.at[0], stored_raw.at[core], (p, sibling)))
    got_in = go(remote(
        w_in_hbm.at[0, :, :, pl.ds(theirs, half)], w_in_raw.at[core], (p, sibling)))

    z_place = [remote(place.at[w], landed_place.at[w], (z_to[w], e)) for w in range(2)]
    z_early = [
        remote(early.at[w], landed.at[w, pl.ds(rows, all_tokens - rows)], (z_to[w], e))
        for w in range(2)]
    for w in range(2):
        @pl.when(valid(z_to[w]))
        def _():
            z_place[w].start()
            z_early[w].start()

    load_out.wait()
    got_out.wait_recv()
    hid_base = take(len(BLOCKS))

    def swap(i, there):
        return pltpu.make_async_remote_copy(
            src_ref=hid_send.at[i], dst_ref=hid_recv.at[there],
            send_sem=send_sem.at[hid_base + i], recv_sem=recv_sem.at[hid_base + there],
            device_id=(p, sibling), device_id_type=MESH)

    def hidden(block):
        i = number(block)
        w_out = w_out_chip[...].reshape(-1, half)
        hid_send[i] = lax.dot_general(
            x_block[i], w_out, (((1,), (1,)), ((), ())), preferred_element_type=F32)
        pending.append(swap(i, number((block[0], block[2], block[1]))))
        pending[-1].start()

    def finish(block):
        i = number(block)
        c, f, s = block
        dx = f + core * (s - f)
        dy = s + core * (f - s)
        at_x = (x // 2) * 2 + (x % 2 + dx) % 2
        at_x = at_x + c * (3 - 2 * at_x)
        chip = at_x * 2 + (y + dy) % 2
        chip_rows = pl.ds(pl.multiple_of(chip * rows, 16), rows)
        swap(i, i).wait_recv()
        slot_gate = jnp.sum(jnp.where(slot_eye, x_gate[i, 0:1, :], 0.0), axis=1, keepdims=True)
        total = (hid_send[i] + hid_recv[i]) * slot_gate
        parts = []
        for h in range(2):
            width = total.shape[1] // 2
            grad = total[:, h * width:(h + 1) * width]
            a = stored_chip[h, 0, chip_rows, :].astype(F32)
            b = stored_chip[h, 1, chip_rows, :].astype(F32)
            squashed = jax.nn.sigmoid(a)
            parts.append((grad * b * squashed * (1.0 + a * (1.0 - squashed))).astype(BF16))
            parts.append((grad * a * squashed).astype(BF16))
        pre = jnp.concatenate(parts, axis=1)
        value = jnp.dot(pre, w_in_chip[...].reshape(-1, half), preferred_element_type=F32)
        acc[i] = value

    def block_of(c, f, s):
        flip = lambda bit, turn: 1 - turn if bit else turn
        return c * 4 + flip(f, turn_first) * 2 + flip(s, turn_second)

    got_ret, got_first = {}, {}

    def send_second(c, f):
        ret_send[c * 2 + f] = acc[block_of(c, f, 1)].astype(BF16)
        got_ret[c, f] = in_pieces(
            pieces, ret_send.at[c * 2 + f], ret_sec.at[c * 2 + f], second)

    def send_first(c):
        got_first[c] = []
        for k, (start, count) in enumerate(pieces):
            span = pl.ds(start, count)
            got_ret[c, 1][k].wait_recv()
            first_send[c, span] = (
                acc[block_of(c, 1, 0), span] + ret_sec[c * 2 + 1, span].astype(F32)).astype(BF16)
            got_first[c].append(go(remote(
                first_send.at[c, span], ret_first.at[c, span], (p, first))))

    def summed(c, k):
        span = pl.ds(*pieces[k])
        got_ret[c, 0][k].wait_recv()
        i = block_of(c, 0, 0)
        part = acc[i, span] + ret_sec[c * 2, span].astype(F32)
        got_first[c][k].wait_recv()
        total = part + ret_first[c, span].astype(F32)
        final[c, span] = (x_block[i, span].astype(F32) + total).astype(BF16)
        return final.at[c, span]

    def arrive(block):
        if block not in arrived:
            for copy in got_x[block]:
                copy.wait_recv()
            got_gate[block].wait_recv()
            arrived.add(block)
        hidden(block)

    hidden((0, 0, 0))
    load_stored.wait()
    got_stored.wait_recv()
    load_in.wait()
    got_in.wait_recv()
    for h in range(2):
        hidden_units = stored_chip.shape[3]
        stored_chip[h] = jnp.transpose(
            stored_raw[h].reshape(-1, 2, hidden_units), (1, 0, 2))
        w_in_chip[h] = jnp.transpose(w_in_raw[h], (1, 0, 2))
    forward((1, 0, 0), "first", "second")
    hidden((1, 0, 0))
    arrive((0, 1, 0))
    arrive((0, 0, 1))
    finish((0, 0, 0))
    finish((1, 0, 0))
    forward((1, 1, 0), "second")
    forward((0, 1, 0), "second")
    hidden((1, 1, 0))
    arrive((1, 0, 1))
    finish((1, 0, 1))
    finish((1, 1, 0))
    finish((0, 1, 0))
    arrive((1, 1, 1))
    finish((1, 1, 1))
    send_second(1, 1)
    send_second(1, 0)
    finish((0, 0, 1))
    arrive((0, 1, 1))
    finish((0, 1, 1))
    send_second(0, 1)
    send_second(0, 0)

    send_first(1)
    got_cut = []
    for k, (start, count) in enumerate(pieces):
        got_cut.append(go(remote(summed(1, k), ret_cut.at[pl.ds(start, count)], (p, cut))))
    send_first(0)

    z_late = [[], []]

    def relay(w, k, rows_ref):
        copy = remote(rows_ref, landed.at[w, pl.ds(*pieces[k])], (z_to[w], late_to[w]))
        z_late[w].append(copy)

        @pl.when(valid(z_to[w]))
        def _():
            copy.start()

    for k in range(len(pieces)):
        got_cut[k].wait_recv()
        relay(1, k, ret_cut.at[pl.ds(*pieces[k])])
    for k in range(len(pieces)):
        relay(0, k, summed(0, k))

    eye = iota((all_tokens, all_tokens), 0) == iota((all_tokens, all_tokens), 1)
    stores = []
    for w in (1, 0):
        @pl.when(valid(z_from[w]))
        def _():
            z_place[w].wait_recv()
            z_early[w].wait_recv()
            position = jnp.sum(
                jnp.where(eye, landed_place[w, 0:1, :], 0.0), axis=1, keepdims=True)
            select = jnp.where(
                iota((all_tokens, all_tokens), 1) == position, 1.0, 0.0).astype(BF16)
            for copy in z_late[w]:
                copy.wait_recv()
            value = jnp.dot(select, landed[w], preferred_element_type=F32).astype(BF16)
            stage[w, 0] = value[:tokens]
            stage[w, 1] = value[tokens:]

        @pl.when(jnp.logical_not(valid(z_from[w])))
        def _():
            stage[w] = jnp.zeros_like(stage[w])

        target = out_hbm.at[directions[w], :, pl.ds(mine, half)]
        stores.append(go(remote(stage.at[w, 1 - core], target, (p, sibling))).wait_recv)
        stores.append(local(stage.at[w, core], target).wait)

    for wait in stores:
        wait()
    for copy in pending:
        copy.wait_send()
    for w in range(2):
        @pl.when(valid(z_to[w]))
        def _():
            for copy in [z_place[w], z_early[w]] + z_late[w]:
                copy.wait_send()


def on_device(n_pipe, grad_out, route_slot, gate_weight, stored_pre, w_in, w_out):
    _, sources, capacity, _, hidden = stored_pre.shape
    _, tokens, features = grad_out.shape
    half, rows, chips = features // 2, 2 * capacity, sources // 2
    hbm = pl.BlockSpec(memory_space=pltpu.HBM)
    vmem = pl.BlockSpec(memory_space=pltpu.VMEM)
    half_rows = (rows, half)
    return pl.pallas_call(
        functools.partial(kernel, n_pipe, capacity),
        out_shape=jax.ShapeDtypeStruct(grad_out.shape, BF16),
        in_specs=[hbm, vmem, vmem, hbm, hbm, hbm],
        out_specs=hbm,
        scratch_shapes=[
            pltpu.VMEM((2, 2, tokens, half), BF16),
            pltpu.VMEM((2, 8, 2 * tokens), F32),
            pltpu.VMEM((2, hidden, half), BF16),
            pltpu.VMEM((2, hidden, 2, half), BF16),
            pltpu.VMEM((2, 2, hidden, half), BF16),
            pltpu.VMEM((2, sources, capacity, 2, hidden), BF16),
            pltpu.VMEM((2, 2, sources * capacity, hidden), BF16),
            pltpu.VMEM(half_rows, BF16),
            pltpu.VMEM((8,) + half_rows, BF16),
            pltpu.VMEM((8, 2 * tokens), F32),
            pltpu.VMEM((8, 8, 2 * tokens), F32),
            pltpu.VMEM((8, rows, 2 * hidden), F32),
            pltpu.VMEM((8, rows, 2 * hidden), F32),
            pltpu.VMEM((8,) + half_rows, F32),
            pltpu.VMEM((4,) + half_rows, BF16),
            pltpu.VMEM((4,) + half_rows, BF16),
            pltpu.VMEM((2,) + half_rows, BF16),
            pltpu.VMEM((2,) + half_rows, BF16),
            pltpu.VMEM((2,) + half_rows, BF16),
            pltpu.VMEM(half_rows, BF16),
            pltpu.VMEM((2, 2 * tokens - rows, half), BF16),
            pltpu.VMEM((2, 8, 2 * tokens), F32),
            pltpu.VMEM((2, 2 * tokens, half), BF16),
            pltpu.VMEM((2, 8, 2 * tokens), F32),
            pltpu.VMEM((2, 2, tokens, half), BF16),
            pltpu.SemaphoreType.DMA((8,)),
            pltpu.SemaphoreType.DMA((COPIES,)),
            pltpu.SemaphoreType.DMA((COPIES,)),
        ],
        compiler_params=pltpu.CompilerParams(
            collective_id=0, has_side_effects=True, vmem_limit_bytes=62 * 2**20),
    )(grad_out, route_slot, gate_weight, stored_pre, w_in, w_out)


def solution(mesh):
    return jax.shard_map(
        functools.partial(on_device, mesh.shape["pipe"]),
        mesh=mesh,
        in_specs=(
            P(None, ("pipe", "expert"), None),
            P(None, ("pipe", "expert")),
            P(None, ("pipe", "expert")),
            P("pipe", None, None, None, "expert"),
            P("pipe", "expert", None, None),
            P("pipe", "expert", None),
        ),
        out_specs=P(None, ("pipe", "expert"), None),
        check_vma=False,
    )
```

```python
import functools

import jax
import jax.numpy as jnp
from jax import lax
from jax.experimental import pallas as pl
from jax.experimental.pallas import tpu as pltpu
from jax.sharding import PartitionSpec as P

MESH = pl.DeviceIdType.MESH
F32, BF16 = jnp.float32, jnp.bfloat16
BLOCKS = [(c, f, s) for c in range(2) for f in range(2) for s in range(2)]


OUT_ROWS, BACK_ROWS = 16, 16
COPIES = 200


def row_pieces(rows, most):
    return [(start, min(most, rows - start)) for start in range(0, rows, most)]


def number(block):
    return block[0] * 4 + block[1] * 2 + block[2]


def iota(shape, dim):
    return lax.broadcasted_iota(jnp.int32, shape, dim).astype(F32)


def kernel(
    n_pipe, capacity,
    grad_hbm, slot_ref, gate_ref, stored_hbm, w_in_hbm, w_out_hbm,
    out_hbm,
    grad_chip, meta, w_out_chip, w_in_raw, w_in_chip, stored_raw, stored_chip,
    cross_block, x_block, cross_gate, x_gate, hid_send, hid_recv, acc, ret_send, ret_sec,
    first_send, ret_first, final, ret_cut, early, place, landed, landed_place, stage,
    local_sem, send_sem, recv_sem,
):
    tokens, half = grad_chip.shape[2:]
    rows, all_tokens = 2 * capacity, 2 * tokens
    out_pieces, pieces = row_pieces(rows, OUT_ROWS), row_pieces(rows, BACK_ROWS)
    p, e = lax.axis_index("pipe"), lax.axis_index("expert")
    core, y, x = e % 2, (e // 2) % 2, e // 4
    g = x // 2
    sibling = e + 1 - 2 * core
    x_next = e + 4 - 8 * (x % 2)
    y_next = e + 2 - 4 * y
    cut = e + 4 * (3 - 2 * x)
    first = x_next + core * (y_next - x_next)
    second = y_next + core * (x_next - y_next)
    z_to = [p - 1 + 2 * g, p + 1 - 2 * g]
    z_from = [z_to[1], z_to[0]]
    directions = [g, 1 - g]

    def valid(rank):
        return jnp.logical_and(rank >= 0, rank < n_pipe)

    counter = [0]

    def take(count=1):
        counter[0] += count
        return counter[0] - count

    def remote(src, dst, device):
        index = take()
        return pltpu.make_async_remote_copy(
            src_ref=src, dst_ref=dst, send_sem=send_sem.at[index], recv_sem=recv_sem.at[index],
            device_id=device, device_id_type=MESH,
        )

    local_counter = [0]

    def local(src, dst):
        local_counter[0] += 1
        copy = pltpu.make_async_copy(src, dst, local_sem.at[local_counter[0] - 1])
        copy.start()
        return copy

    def far(rank):
        ring = n_pipe // 2
        return jnp.logical_and(valid(rank), rank // ring != p // ring)

    is_far = [far(rank).astype(jnp.int32) for rank in z_to]
    late_to = [e + flag * (y_next - e) for flag in is_far]
    turn_first, turn_second = is_far[0] * core, is_far[0] * (1 - core)

    barrier = pltpu.get_barrier_semaphore()
    for other in (sibling, first, second, cut):
        pl.semaphore_signal(barrier, inc=1, device_id=(p, other), device_id_type=MESH)
    for rank in z_to:
        @pl.when(valid(rank))
        def _():
            pl.semaphore_signal(barrier, inc=1, device_id=(rank, e), device_id_type=MESH)

        @pl.when(far(rank))
        def _():
            pl.semaphore_signal(barrier, inc=1, device_id=(rank, y_next), device_id_type=MESH)

    mine = pl.multiple_of(core * half, 128)
    theirs = pl.multiple_of((1 - core) * half, 128)

    load_grad = [None, None]
    for w in (0, 1):
        load_grad[w] = local(
            grad_hbm.at[directions[w], :, pl.ds(mine, half)], grad_chip.at[w, core])

    slot = slot_ref[...].astype(F32)
    gate = gate_ref[...]
    meta[0] = jnp.zeros_like(meta[0])
    meta[0, 0:2, 0:tokens] = slot
    meta[0, 0:2, tokens:all_tokens] = slot
    meta[0, 2:4, 0:tokens] = gate
    meta[0, 2:4, tokens:all_tokens] = gate

    pl.semaphore_wait(
        barrier, 4 + sum(valid(rank).astype(jnp.int32) for rank in z_to) + sum(is_far))

    pending = []

    def go(copy):
        copy.start()
        pending.append(copy)
        return copy

    def in_pieces(spans, src, dst, other):
        return [go(remote(src.at[pl.ds(*span)], dst.at[pl.ds(*span)], (p, other)))
                for span in spans]

    got_meta = go(remote(meta.at[0], meta.at[1], (p, sibling)))
    got_grad = [None, None]
    for w in (0, 1):
        got_grad[w] = go(remote(
            grad_hbm.at[directions[w], :, pl.ds(theirs, half)], grad_chip.at[w, core],
            (p, sibling)))
    got_meta.wait_recv()

    lane = lax.broadcasted_iota(jnp.int32, (1, all_tokens), 1)
    is_own = (lane // tokens) == core
    earlier = jnp.where(
        iota((all_tokens, all_tokens), 0) < iota((all_tokens, all_tokens), 1), 1.0, 0.0
    ).astype(BF16)

    slot_eye = iota((rows, all_tokens), 0) == iota((rows, all_tokens), 1)

    def pack(w):
        row = pl.ds(directions[w], 1)
        gate_row = pl.ds(directions[w] + 2, 1)
        chip_slot = jnp.where(is_own, meta[0, row, :], meta[1, row, :])
        chip_gate = jnp.where(is_own, meta[0, gate_row, :], meta[1, gate_row, :])
        free = jnp.broadcast_to(jnp.where(chip_slot < 0, 1.0, 0.0), (8, all_tokens))
        rank = jnp.dot(free.astype(BF16), earlier, preferred_element_type=F32)[0:1]
        position = jnp.where(
            chip_slot < 0, rank + float(rows),
            chip_slot + jnp.where(lane >= tokens, float(capacity), 0.0))
        place[w] = jnp.broadcast_to(position, place.shape[1:])
        onehot = jnp.where(iota((all_tokens, all_tokens), 0) == position, 1.0, 0.0)
        slot_gate = jnp.sum(onehot[:rows] * chip_gate, axis=1, keepdims=True)
        load_grad[w].wait()
        got_grad[w].wait_recv()
        both = jnp.concatenate([grad_chip[w, 0], grad_chip[w, 1]], axis=0)
        picked = jnp.dot(onehot.astype(BF16), both, preferred_element_type=F32)
        early[w] = picked[rows:].astype(BF16)
        gates = jnp.sum(jnp.where(slot_eye, slot_gate, 0.0), axis=0, keepdims=True)
        return picked[:rows].astype(BF16), jnp.broadcast_to(gates, cross_gate.shape)

    got_x, got_gate, arrived = {}, {}, set()

    def forward(block, *axes):
        c, f, s = block
        targets = {"first": (c, 1, s), "second": (c, f, 1)}
        for axis in axes:
            got_x[targets[axis]] = []
        for k, (start, count) in enumerate(out_pieces):
            span = pl.ds(start, count)
            if block in got_x and block not in arrived:
                got_x[block][k].wait_recv()
            for axis in axes:
                got_x[targets[axis]].append(go(remote(
                    x_block.at[number(block), span], x_block.at[number(targets[axis]), span],
                    (p, first if axis == "first" else second))))
        if block in got_gate and block not in arrived:
            got_gate[block].wait_recv()
        for axis in axes:
            got_gate[targets[axis]] = go(remote(
                x_gate.at[number(block)], x_gate.at[number(targets[axis])],
                (p, first if axis == "first" else second)))
        arrived.add(block)

    x_block[0], x_gate[0] = pack(0)
    forward((0, 0, 0), "first", "second")
    cross_block[...], cross_gate[...] = pack(1)
    got_x[1, 0, 0] = in_pieces(out_pieces, cross_block, x_block.at[number((1, 0, 0))], cut)
    got_gate[1, 0, 0] = go(remote(cross_gate, x_gate.at[number((1, 0, 0))], (p, cut)))

    load_out = local(w_out_hbm.at[0, :, pl.ds(mine, half)], w_out_chip.at[core])
    load_stored = local(stored_hbm.at[0], stored_raw.at[core])
    load_in = local(w_in_hbm.at[0, :, :, pl.ds(mine, half)], w_in_raw.at[core])
    got_out = go(remote(w_out_hbm.at[0, :, pl.ds(theirs, half)], w_out_chip.at[core], (p, sibling)))
    got_stored = go(remote(stored_hbm.at[0], stored_raw.at[core], (p, sibling)))
    got_in = go(remote(
        w_in_hbm.at[0, :, :, pl.ds(theirs, half)], w_in_raw.at[core], (p, sibling)))

    z_place = [remote(place.at[w], landed_place.at[w], (z_to[w], e)) for w in range(2)]
    z_early = [
        remote(early.at[w], landed.at[w, pl.ds(rows, all_tokens - rows)], (z_to[w], e))
        for w in range(2)]
    for w in range(2):
        @pl.when(valid(z_to[w]))
        def _():
            z_place[w].start()
            z_early[w].start()

    load_out.wait()
    got_out.wait_recv()
    hid_base = take(len(BLOCKS))

    def swap(i, there):
        return pltpu.make_async_remote_copy(
            src_ref=hid_send.at[i], dst_ref=hid_recv.at[there],
            send_sem=send_sem.at[hid_base + i], recv_sem=recv_sem.at[hid_base + there],
            device_id=(p, sibling), device_id_type=MESH)

    def hidden(block):
        i = number(block)
        w_out = w_out_chip[...].reshape(-1, half)
        hid_send[i] = lax.dot_general(
            x_block[i], w_out, (((1,), (1,)), ((), ())), preferred_element_type=F32)
        pending.append(swap(i, number((block[0], block[2], block[1]))))
        pending[-1].start()

    def finish(block):
        i = number(block)
        c, f, s = block
        dx = f + core * (s - f)
        dy = s + core * (f - s)
        at_x = (x // 2) * 2 + (x % 2 + dx) % 2
        at_x = at_x + c * (3 - 2 * at_x)
        chip = at_x * 2 + (y + dy) % 2
        chip_rows = pl.ds(pl.multiple_of(chip * rows, 16), rows)
        swap(i, i).wait_recv()
        slot_gate = jnp.sum(jnp.where(slot_eye, x_gate[i, 0:1, :], 0.0), axis=1, keepdims=True)
        total = (hid_send[i] + hid_recv[i]) * slot_gate
        parts = []
        for h in range(2):
            width = total.shape[1] // 2
            grad = total[:, h * width:(h + 1) * width]
            a = stored_chip[h, 0, chip_rows, :].astype(F32)
            b = stored_chip[h, 1, chip_rows, :].astype(F32)
            squashed = jax.nn.sigmoid(a)
            parts.append((grad * b * squashed * (1.0 + a * (1.0 - squashed))).astype(BF16))
            parts.append((grad * a * squashed).astype(BF16))
        pre = jnp.concatenate(parts, axis=1)
        value = jnp.dot(pre, w_in_chip[...].reshape(-1, half), preferred_element_type=F32)
        acc[i] = value

    def block_of(c, f, s):
        flip = lambda bit, turn: 1 - turn if bit else turn
        return c * 4 + flip(f, turn_first) * 2 + flip(s, turn_second)

    got_ret, got_first = {}, {}

    def send_second(c, f):
        ret_send[c * 2 + f] = acc[block_of(c, f, 1)].astype(BF16)
        got_ret[c, f] = in_pieces(
            pieces, ret_send.at[c * 2 + f], ret_sec.at[c * 2 + f], second)

    def send_first(c):
        got_first[c] = []
        for k, (start, count) in enumerate(pieces):
            span = pl.ds(start, count)
            got_ret[c, 1][k].wait_recv()
            first_send[c, span] = (
                acc[block_of(c, 1, 0), span] + ret_sec[c * 2 + 1, span].astype(F32)).astype(BF16)
            got_first[c].append(go(remote(
                first_send.at[c, span], ret_first.at[c, span], (p, first))))

    def summed(c, k):
        span = pl.ds(*pieces[k])
        got_ret[c, 0][k].wait_recv()
        i = block_of(c, 0, 0)
        part = acc[i, span] + ret_sec[c * 2, span].astype(F32)
        got_first[c][k].wait_recv()
        total = part + ret_first[c, span].astype(F32)
        final[c, span] = (x_block[i, span].astype(F32) + total).astype(BF16)
        return final.at[c, span]

    def arrive(block):
        if block not in arrived:
            for copy in got_x[block]:
                copy.wait_recv()
            got_gate[block].wait_recv()
            arrived.add(block)
        hidden(block)

    hidden((0, 0, 0))
    load_stored.wait()
    got_stored.wait_recv()
    load_in.wait()
    got_in.wait_recv()
    for h in range(2):
        hidden_units = stored_chip.shape[3]
        stored_chip[h] = jnp.transpose(
            stored_raw[h].reshape(-1, 2, hidden_units), (1, 0, 2))
        w_in_chip[h] = jnp.transpose(w_in_raw[h], (1, 0, 2))
    forward((1, 0, 0), "first", "second")
    hidden((1, 0, 0))
    arrive((0, 1, 0))
    arrive((0, 0, 1))
    finish((0, 0, 0))
    finish((1, 0, 0))
    forward((1, 1, 0), "second")
    forward((0, 1, 0), "second")
    hidden((1, 1, 0))
    arrive((1, 0, 1))
    finish((1, 0, 1))
    finish((1, 1, 0))
    finish((0, 1, 0))
    arrive((1, 1, 1))
    finish((1, 1, 1))
    send_second(1, 1)
    send_second(1, 0)
    finish((0, 0, 1))
    arrive((0, 1, 1))
    finish((0, 1, 1))
    send_second(0, 1)
    send_second(0, 0)

    send_first(1)
    got_cut = []
    for k, (start, count) in enumerate(pieces):
        got_cut.append(go(remote(summed(1, k), ret_cut.at[pl.ds(start, count)], (p, cut))))
    send_first(0)

    z_late = [[], []]

    def relay(w, k, rows_ref):
        copy = remote(rows_ref, landed.at[w, pl.ds(*pieces[k])], (z_to[w], late_to[w]))
        z_late[w].append(copy)

        @pl.when(valid(z_to[w]))
        def _():
            copy.start()

    for k in range(len(pieces)):
        got_cut[k].wait_recv()
        relay(1, k, ret_cut.at[pl.ds(*pieces[k])])
    for k in range(len(pieces)):
        relay(0, k, summed(0, k))

    eye = iota((all_tokens, all_tokens), 0) == iota((all_tokens, all_tokens), 1)
    stores = []
    for w in (1, 0):
        @pl.when(valid(z_from[w]))
        def _():
            z_place[w].wait_recv()
            z_early[w].wait_recv()
            position = jnp.sum(
                jnp.where(eye, landed_place[w, 0:1, :], 0.0), axis=1, keepdims=True)
            select = jnp.where(
                iota((all_tokens, all_tokens), 1) == position, 1.0, 0.0).astype(BF16)
            for copy in z_late[w]:
                copy.wait_recv()
            value = jnp.dot(select, landed[w], preferred_element_type=F32).astype(BF16)
            stage[w, 0] = value[:tokens]
            stage[w, 1] = value[tokens:]

        @pl.when(jnp.logical_not(valid(z_from[w])))
        def _():
            stage[w] = jnp.zeros_like(stage[w])

        target = out_hbm.at[directions[w], :, pl.ds(mine, half)]
        stores.append(go(remote(stage.at[w, 1 - core], target, (p, sibling))).wait_recv)
        stores.append(local(stage.at[w, core], target).wait)

    for wait in stores:
        wait()
    for copy in pending:
        copy.wait_send()
    for w in range(2):
        @pl.when(valid(z_to[w]))
        def _():
            for copy in [z_place[w], z_early[w]] + z_late[w]:
                copy.wait_send()


def on_device(n_pipe, grad_out, route_slot, gate_weight, stored_pre, w_in, w_out):
    _, sources, capacity, _, hidden = stored_pre.shape
    _, tokens, features = grad_out.shape
    half, rows, chips = features // 2, 2 * capacity, sources // 2
    hbm = pl.BlockSpec(memory_space=pltpu.HBM)
    vmem = pl.BlockSpec(memory_space=pltpu.VMEM)
    half_rows = (rows, half)
    return pl.pallas_call(
        functools.partial(kernel, n_pipe, capacity),
        out_shape=pltpu.VMEM(grad_out.shape, BF16),
        in_specs=[hbm, vmem, vmem, hbm, hbm, hbm],
        out_specs=vmem,
        scratch_shapes=[
            pltpu.VMEM((2, 2, tokens, half), BF16),
            pltpu.VMEM((2, 8, 2 * tokens), F32),
            pltpu.VMEM((2, hidden, half), BF16),
            pltpu.VMEM((2, hidden, 2, half), BF16),
            pltpu.VMEM((2, 2, hidden, half), BF16),
            pltpu.VMEM((2, sources, capacity, 2, hidden), BF16),
            pltpu.VMEM((2, 2, sources * capacity, hidden), BF16),
            pltpu.VMEM(half_rows, BF16),
            pltpu.VMEM((8,) + half_rows, BF16),
            pltpu.VMEM((8, 2 * tokens), F32),
            pltpu.VMEM((8, 8, 2 * tokens), F32),
            pltpu.VMEM((8, rows, 2 * hidden), F32),
            pltpu.VMEM((8, rows, 2 * hidden), F32),
            pltpu.VMEM((8,) + half_rows, F32),
            pltpu.VMEM((4,) + half_rows, BF16),
            pltpu.VMEM((4,) + half_rows, BF16),
            pltpu.VMEM((2,) + half_rows, BF16),
            pltpu.VMEM((2,) + half_rows, BF16),
            pltpu.VMEM((2,) + half_rows, BF16),
            pltpu.VMEM(half_rows, BF16),
            pltpu.VMEM((2, 2 * tokens - rows, half), BF16),
            pltpu.VMEM((2, 8, 2 * tokens), F32),
            pltpu.VMEM((2, 2 * tokens, half), BF16),
            pltpu.VMEM((2, 8, 2 * tokens), F32),
            pltpu.VMEM((2, 2, tokens, half), BF16),
            pltpu.SemaphoreType.DMA((8,)),
            pltpu.SemaphoreType.DMA((COPIES,)),
            pltpu.SemaphoreType.DMA((COPIES,)),
        ],
        compiler_params=pltpu.CompilerParams(
            collective_id=0, has_side_effects=True, vmem_limit_bytes=56 * 2**20),
    )(grad_out, route_slot, gate_weight, stored_pre, w_in, w_out)


def solution(mesh):
    return jax.shard_map(
        functools.partial(on_device, mesh.shape["pipe"]),
        mesh=mesh,
        in_specs=(
            P(None, ("pipe", "expert"), None),
            P(None, ("pipe", "expert")),
            P(None, ("pipe", "expert")),
            P("pipe", None, None, None, "expert"),
            P("pipe", "expert", None, None),
            P("pipe", "expert", None),
        ),
        out_specs=P(None, ("pipe", "expert"), None),
        check_vma=False,
    )
```

```python
import functools

import jax
import jax.numpy as jnp
from jax import lax
from jax.experimental import pallas as pl
from jax.experimental.pallas import tpu as pltpu
from jax.sharding import PartitionSpec as P

MESH = pl.DeviceIdType.MESH
F32, BF16 = jnp.float32, jnp.bfloat16
BLOCKS = [(c, f, s) for c in range(2) for f in range(2) for s in range(2)]


OUT_ROWS, BACK_ROWS = 16, 16
COPIES = 200


def row_pieces(rows, most):
    return [(start, min(most, rows - start)) for start in range(0, rows, most)]


def number(block):
    return block[0] * 4 + block[1] * 2 + block[2]


def iota(shape, dim):
    return lax.broadcasted_iota(jnp.int32, shape, dim).astype(F32)


def kernel(
    n_pipe, capacity,
    grad_hbm, slot_ref, gate_ref, stored_hbm, w_in_hbm, w_out_hbm,
    out_hbm,
    grad_chip, meta, w_out_chip, w_in_raw, w_in_chip, stored_raw, stored_chip,
    cross_block, x_block, cross_gate, x_gate, hid_send, hid_recv, acc, ret_send, ret_sec,
    first_send, ret_first, final, ret_cut, early, place, landed, landed_place, stage,
    local_sem, send_sem, recv_sem,
):
    tokens, half = grad_chip.shape[2:]
    rows, all_tokens = 2 * capacity, 2 * tokens
    out_pieces, pieces = row_pieces(rows, OUT_ROWS), row_pieces(rows, BACK_ROWS)
    p, e = lax.axis_index("pipe"), lax.axis_index("expert")
    core, y, x = e % 2, (e // 2) % 2, e // 4
    g = x // 2
    sibling = e + 1 - 2 * core
    x_next = e + 4 - 8 * (x % 2)
    y_next = e + 2 - 4 * y
    cut = e + 4 * (3 - 2 * x)
    first = x_next + core * (y_next - x_next)
    second = y_next + core * (x_next - y_next)
    z_to = [p - 1 + 2 * g, p + 1 - 2 * g]
    z_from = [z_to[1], z_to[0]]
    directions = [g, 1 - g]

    def valid(rank):
        return jnp.logical_and(rank >= 0, rank < n_pipe)

    counter = [0]

    def take(count=1):
        counter[0] += count
        return counter[0] - count

    def remote(src, dst, device):
        index = take()
        return pltpu.make_async_remote_copy(
            src_ref=src, dst_ref=dst, send_sem=send_sem.at[index], recv_sem=recv_sem.at[index],
            device_id=device, device_id_type=MESH,
        )

    local_counter = [0]

    def local(src, dst):
        local_counter[0] += 1
        copy = pltpu.make_async_copy(src, dst, local_sem.at[local_counter[0] - 1])
        copy.start()
        return copy

    def far(rank):
        ring = n_pipe // 2
        return jnp.logical_and(valid(rank), rank // ring != p // ring)

    is_far = [far(rank).astype(jnp.int32) for rank in z_to]
    late_to = [e + flag * (y_next - e) for flag in is_far]
    turn_first, turn_second = is_far[0] * core, is_far[0] * (1 - core)

    barrier = pltpu.get_barrier_semaphore()
    for other in (sibling, first, second, cut):
        pl.semaphore_signal(barrier, inc=1, device_id=(p, other), device_id_type=MESH)
    for rank in z_to:
        @pl.when(valid(rank))
        def _():
            pl.semaphore_signal(barrier, inc=1, device_id=(rank, e), device_id_type=MESH)

        @pl.when(far(rank))
        def _():
            pl.semaphore_signal(barrier, inc=1, device_id=(rank, y_next), device_id_type=MESH)

    mine = pl.multiple_of(core * half, 128)
    theirs = pl.multiple_of((1 - core) * half, 128)

    load_grad = [None, None]
    for w in (0, 1):
        load_grad[w] = local(
            grad_hbm.at[directions[w], :, pl.ds(mine, half)], grad_chip.at[w, core])

    slot = slot_ref[...].astype(F32)
    gate = gate_ref[...]
    meta[0] = jnp.zeros_like(meta[0])
    meta[0, 0:2, 0:tokens] = slot
    meta[0, 0:2, tokens:all_tokens] = slot
    meta[0, 2:4, 0:tokens] = gate
    meta[0, 2:4, tokens:all_tokens] = gate

    pl.semaphore_wait(
        barrier, 4 + sum(valid(rank).astype(jnp.int32) for rank in z_to) + sum(is_far))

    pending = []

    def go(copy):
        copy.start()
        pending.append(copy)
        return copy

    def in_pieces(spans, src, dst, other):
        return [go(remote(src.at[pl.ds(*span)], dst.at[pl.ds(*span)], (p, other)))
                for span in spans]

    got_meta = go(remote(meta.at[0], meta.at[1], (p, sibling)))
    got_grad = [None, None]
    for w in (0, 1):
        got_grad[w] = go(remote(
            grad_hbm.at[directions[w], :, pl.ds(theirs, half)], grad_chip.at[w, core],
            (p, sibling)))
    got_meta.wait_recv()

    lane = lax.broadcasted_iota(jnp.int32, (1, all_tokens), 1)
    is_own = (lane // tokens) == core
    earlier = jnp.where(
        iota((all_tokens, all_tokens), 0) < iota((all_tokens, all_tokens), 1), 1.0, 0.0
    ).astype(BF16)

    slot_eye = iota((rows, all_tokens), 0) == iota((rows, all_tokens), 1)

    def pack(w):
        row = pl.ds(directions[w], 1)
        gate_row = pl.ds(directions[w] + 2, 1)
        chip_slot = jnp.where(is_own, meta[0, row, :], meta[1, row, :])
        chip_gate = jnp.where(is_own, meta[0, gate_row, :], meta[1, gate_row, :])
        free = jnp.broadcast_to(jnp.where(chip_slot < 0, 1.0, 0.0), (8, all_tokens))
        rank = jnp.dot(free.astype(BF16), earlier, preferred_element_type=F32)[0:1]
        position = jnp.where(
            chip_slot < 0, rank + float(rows),
            chip_slot + jnp.where(lane >= tokens, float(capacity), 0.0))
        place[w] = jnp.broadcast_to(position, place.shape[1:])
        onehot = jnp.where(iota((all_tokens, all_tokens), 0) == position, 1.0, 0.0)
        slot_gate = jnp.sum(onehot[:rows] * chip_gate, axis=1, keepdims=True)
        load_grad[w].wait()
        got_grad[w].wait_recv()
        both = jnp.concatenate([grad_chip[w, 0], grad_chip[w, 1]], axis=0)
        picked = jnp.dot(onehot.astype(BF16), both, preferred_element_type=F32)
        early[w] = picked[rows:].astype(BF16)
        gates = jnp.sum(jnp.where(slot_eye, slot_gate, 0.0), axis=0, keepdims=True)
        return picked[:rows].astype(BF16), jnp.broadcast_to(gates, cross_gate.shape)

    got_x, got_gate, arrived = {}, {}, set()

    def forward(block, *axes):
        c, f, s = block
        targets = {"first": (c, 1, s), "second": (c, f, 1)}
        for axis in axes:
            got_x[targets[axis]] = []
        for k, (start, count) in enumerate(out_pieces):
            span = pl.ds(start, count)
            if block in got_x and block not in arrived:
                got_x[block][k].wait_recv()
            for axis in axes:
                got_x[targets[axis]].append(go(remote(
                    x_block.at[number(block), span], x_block.at[number(targets[axis]), span],
                    (p, first if axis == "first" else second))))
        if block in got_gate and block not in arrived:
            got_gate[block].wait_recv()
        for axis in axes:
            got_gate[targets[axis]] = go(remote(
                x_gate.at[number(block)], x_gate.at[number(targets[axis])],
                (p, first if axis == "first" else second)))
        arrived.add(block)

    x_block[0], x_gate[0] = pack(0)
    forward((0, 0, 0), "first", "second")
    cross_block[...], cross_gate[...] = pack(1)
    got_x[1, 0, 0] = in_pieces(out_pieces, cross_block, x_block.at[number((1, 0, 0))], cut)
    got_gate[1, 0, 0] = go(remote(cross_gate, x_gate.at[number((1, 0, 0))], (p, cut)))

    load_out = local(w_out_hbm.at[0, :, pl.ds(mine, half)], w_out_chip.at[core])
    load_stored = local(stored_hbm.at[0], stored_raw.at[core])
    load_in = local(w_in_hbm.at[0, :, :, pl.ds(mine, half)], w_in_raw.at[core])
    got_out = go(remote(w_out_hbm.at[0, :, pl.ds(theirs, half)], w_out_chip.at[core], (p, sibling)))
    got_stored = go(remote(stored_hbm.at[0], stored_raw.at[core], (p, sibling)))
    got_in = go(remote(
        w_in_hbm.at[0, :, :, pl.ds(theirs, half)], w_in_raw.at[core], (p, sibling)))

    z_place = [remote(place.at[w], landed_place.at[w], (z_to[w], e)) for w in range(2)]
    z_early = [
        remote(early.at[w], landed.at[w, pl.ds(rows, all_tokens - rows)], (z_to[w], e))
        for w in range(2)]
    for w in range(2):
        @pl.when(valid(z_to[w]))
        def _():
            z_place[w].start()
            z_early[w].start()

    load_out.wait()
    got_out.wait_recv()
    hid_base = take(len(BLOCKS))

    def swap(i, there):
        return pltpu.make_async_remote_copy(
            src_ref=hid_send.at[i], dst_ref=hid_recv.at[there],
            send_sem=send_sem.at[hid_base + i], recv_sem=recv_sem.at[hid_base + there],
            device_id=(p, sibling), device_id_type=MESH)

    def hidden(block):
        i = number(block)
        w_out = w_out_chip[...].reshape(-1, half)
        hid_send[i] = lax.dot_general(
            x_block[i], w_out, (((1,), (1,)), ((), ())), preferred_element_type=F32)
        pending.append(swap(i, number((block[0], block[2], block[1]))))
        pending[-1].start()

    def finish(block):
        i = number(block)
        c, f, s = block
        dx = f + core * (s - f)
        dy = s + core * (f - s)
        at_x = (x // 2) * 2 + (x % 2 + dx) % 2
        at_x = at_x + c * (3 - 2 * at_x)
        chip = at_x * 2 + (y + dy) % 2
        chip_rows = pl.ds(pl.multiple_of(chip * rows, 16), rows)
        swap(i, i).wait_recv()
        slot_gate = jnp.sum(jnp.where(slot_eye, x_gate[i, 0:1, :], 0.0), axis=1, keepdims=True)
        total = (hid_send[i] + hid_recv[i]) * slot_gate
        parts = []
        for h in range(2):
            width = total.shape[1] // 2
            grad = total[:, h * width:(h + 1) * width]
            a = stored_chip[h, 0, chip_rows, :].astype(F32)
            b = stored_chip[h, 1, chip_rows, :].astype(F32)
            squashed = jax.nn.sigmoid(a)
            parts.append((grad * b * squashed * (1.0 + a * (1.0 - squashed))).astype(BF16))
            parts.append((grad * a * squashed).astype(BF16))
        pre = jnp.concatenate(parts, axis=1)
        value = jnp.dot(pre, w_in_chip[...].reshape(-1, half), preferred_element_type=F32)
        acc[i] = value

    def block_of(c, f, s):
        flip = lambda bit, turn: 1 - turn if bit else turn
        return c * 4 + flip(f, turn_first) * 2 + flip(s, turn_second)

    got_ret, got_first = {}, {}

    def send_second(c, f):
        ret_send[c * 2 + f] = acc[block_of(c, f, 1)].astype(BF16)
        got_ret[c, f] = in_pieces(
            pieces, ret_send.at[c * 2 + f], ret_sec.at[c * 2 + f], second)

    def send_first(c):
        got_first[c] = []
        for k, (start, count) in enumerate(pieces):
            span = pl.ds(start, count)
            got_ret[c, 1][k].wait_recv()
            first_send[c, span] = (
                acc[block_of(c, 1, 0), span] + ret_sec[c * 2 + 1, span].astype(F32)).astype(BF16)
            got_first[c].append(go(remote(
                first_send.at[c, span], ret_first.at[c, span], (p, first))))

    def summed(c, k):
        span = pl.ds(*pieces[k])
        got_ret[c, 0][k].wait_recv()
        i = block_of(c, 0, 0)
        part = acc[i, span] + ret_sec[c * 2, span].astype(F32)
        got_first[c][k].wait_recv()
        total = part + ret_first[c, span].astype(F32)
        final[c, span] = (x_block[i, span].astype(F32) + total).astype(BF16)
        return final.at[c, span]

    def arrive(block):
        if block not in arrived:
            for copy in got_x[block]:
                copy.wait_recv()
            got_gate[block].wait_recv()
            arrived.add(block)
        hidden(block)

    hidden((0, 0, 0))
    load_stored.wait()
    got_stored.wait_recv()
    load_in.wait()
    got_in.wait_recv()
    for h in range(2):
        hidden_units = stored_chip.shape[3]
        stored_chip[h] = jnp.transpose(
            stored_raw[h].reshape(-1, 2, hidden_units), (1, 0, 2))
        w_in_chip[h] = jnp.transpose(w_in_raw[h], (1, 0, 2))
    forward((1, 0, 0), "first", "second")
    hidden((1, 0, 0))
    arrive((0, 1, 0))
    arrive((0, 0, 1))
    finish((0, 0, 0))
    finish((1, 0, 0))
    forward((1, 1, 0), "second")
    forward((0, 1, 0), "second")
    hidden((1, 1, 0))
    arrive((1, 0, 1))
    finish((1, 0, 1))
    finish((1, 1, 0))
    finish((0, 1, 0))
    arrive((1, 1, 1))
    finish((1, 1, 1))
    send_second(1, 1)
    send_second(1, 0)
    finish((0, 0, 1))
    arrive((0, 1, 1))
    finish((0, 1, 1))
    send_second(0, 1)
    send_second(0, 0)

    send_first(1)
    got_cut = []
    for k, (start, count) in enumerate(pieces):
        got_cut.append(go(remote(summed(1, k), ret_cut.at[pl.ds(start, count)], (p, cut))))
    send_first(0)

    z_late = [[], []]

    def relay(w, k, rows_ref):
        copy = remote(rows_ref, landed.at[w, pl.ds(*pieces[k])], (z_to[w], late_to[w]))
        z_late[w].append(copy)

        @pl.when(valid(z_to[w]))
        def _():
            copy.start()

    for k in range(len(pieces)):
        got_cut[k].wait_recv()
        relay(1, k, ret_cut.at[pl.ds(*pieces[k])])
    for k in range(len(pieces)):
        relay(0, k, summed(0, k))

    stores = []
    for w in (1, 0):
        target = out_hbm.at[directions[w], :, pl.ds(mine, half)]
        for owner in (1 - core, core):
            @pl.when(valid(z_from[w]))
            def _():
                if owner is not core:
                    z_place[w].wait_recv()
                    z_early[w].wait_recv()
                shape = (tokens, all_tokens)
                token = iota(shape, 0) + (owner * tokens).astype(F32)
                position = jnp.sum(
                    jnp.where(token == iota(shape, 1), landed_place[w, 0:1, :], 0.0),
                    axis=1, keepdims=True)
                select = jnp.where(iota(shape, 1) == position, 1.0, 0.0).astype(BF16)
                if owner is not core:
                    for copy in z_late[w]:
                        copy.wait_recv()
                stage[w, owner] = jnp.dot(
                    select, landed[w], preferred_element_type=F32).astype(BF16)

            @pl.when(jnp.logical_not(valid(z_from[w])))
            def _():
                stage[w, owner] = jnp.zeros(stage.shape[2:], BF16)

            if owner is core:
                stores.append(local(stage.at[w, owner], target).wait)
            else:
                stores.append(go(remote(stage.at[w, owner], target, (p, sibling))).wait_recv)

    for wait in stores:
        wait()
    for copy in pending:
        copy.wait_send()
    for w in range(2):
        @pl.when(valid(z_to[w]))
        def _():
            for copy in [z_place[w], z_early[w]] + z_late[w]:
                copy.wait_send()


def on_device(n_pipe, grad_out, route_slot, gate_weight, stored_pre, w_in, w_out):
    _, sources, capacity, _, hidden = stored_pre.shape
    _, tokens, features = grad_out.shape
    half, rows, chips = features // 2, 2 * capacity, sources // 2
    hbm = pl.BlockSpec(memory_space=pltpu.HBM)
    vmem = pl.BlockSpec(memory_space=pltpu.VMEM)
    half_rows = (rows, half)
    return pl.pallas_call(
        functools.partial(kernel, n_pipe, capacity),
        out_shape=pltpu.VMEM(grad_out.shape, BF16),
        in_specs=[hbm, vmem, vmem, hbm, hbm, hbm],
        out_specs=vmem,
        scratch_shapes=[
            pltpu.VMEM((2, 2, tokens, half), BF16),
            pltpu.VMEM((2, 8, 2 * tokens), F32),
            pltpu.VMEM((2, hidden, half), BF16),
            pltpu.VMEM((2, hidden, 2, half), BF16),
            pltpu.VMEM((2, 2, hidden, half), BF16),
            pltpu.VMEM((2, sources, capacity, 2, hidden), BF16),
            pltpu.VMEM((2, 2, sources * capacity, hidden), BF16),
            pltpu.VMEM(half_rows, BF16),
            pltpu.VMEM((8,) + half_rows, BF16),
            pltpu.VMEM((8, 2 * tokens), F32),
            pltpu.VMEM((8, 8, 2 * tokens), F32),
            pltpu.VMEM((8, rows, 2 * hidden), F32),
            pltpu.VMEM((8, rows, 2 * hidden), F32),
            pltpu.VMEM((8,) + half_rows, F32),
            pltpu.VMEM((4,) + half_rows, BF16),
            pltpu.VMEM((4,) + half_rows, BF16),
            pltpu.VMEM((2,) + half_rows, BF16),
            pltpu.VMEM((2,) + half_rows, BF16),
            pltpu.VMEM((2,) + half_rows, BF16),
            pltpu.VMEM(half_rows, BF16),
            pltpu.VMEM((2, 2 * tokens - rows, half), BF16),
            pltpu.VMEM((2, 8, 2 * tokens), F32),
            pltpu.VMEM((2, 2 * tokens, half), BF16),
            pltpu.VMEM((2, 8, 2 * tokens), F32),
            pltpu.VMEM((2, 2, tokens, half), BF16),
            pltpu.SemaphoreType.DMA((8,)),
            pltpu.SemaphoreType.DMA((COPIES,)),
            pltpu.SemaphoreType.DMA((COPIES,)),
        ],
        compiler_params=pltpu.CompilerParams(
            collective_id=0, has_side_effects=True, vmem_limit_bytes=56 * 2**20),
    )(grad_out, route_slot, gate_weight, stored_pre, w_in, w_out)


def solution(mesh):
    return jax.shard_map(
        functools.partial(on_device, mesh.shape["pipe"]),
        mesh=mesh,
        in_specs=(
            P(None, ("pipe", "expert"), None),
            P(None, ("pipe", "expert")),
            P(None, ("pipe", "expert")),
            P("pipe", None, None, None, "expert"),
            P("pipe", "expert", None, None),
            P("pipe", "expert", None),
        ),
        out_specs=P(None, ("pipe", "expert"), None),
        check_vma=False,
    )
```
